128 devices in a mesh: row: 8 (over z, core), col: 16 (over x, y).
Axes of the slice: x: 4, y: 4, z: 4, core: 2. Of those that a mesh axis runs over, the one named last changes fastest.
Arguments:
- tile_blocks: bfloat16 [65536, 128, 128], P(('row', 'col')), may hold values from -0.1875 to 0.1875
- tile_column: int32 [65536], P(('row', 'col')), may hold values from 0 to 4095, as said below
- row_degree: int32 [4096], P(('row', 'col')), may hold values from 1 to 16, as said below
- node_weight: float32 [524288], P(('row', 'col')), may hold values from 1 to 50
- block_now: float32 [524288, 64], P(('row', 'col')), may hold values from -6 to 6
- block_prev: float32 [524288, 64], P(('row', 'col')), may hold values from -6 to 6
- coupling: float32 [64, 64], replicated, may hold values from -0.75 to 0.75
Outputs:
- block_next: float32 [524288, 64], P(('row', 'col'))
- rayleigh: float32 [64, 64], replicated
- r_factor: float32 [64, 64], replicated
The draws below stay inside these ranges and needn't reach their ends.
Inputs may be any that keep to these rules, and one draw needn't show every extreme that they name: `tile_column`: the tile column of a slot lies in the slab of a device with the same col index as the slot's device. `row_degree`: in every draw one device has all its tile rows at 16 tiles.
All inputs are finite; a program needn't handle non-finite values.
Results may differ from the reference program's by a relative error of at most 0.00047.
Values may be sent and summed in bfloat16 or wider, within the bound.
No kernel may reach another device: no remote copies, remote signals or barrier semaphores. Data moves between devices by JAX's collectives and lax.ppermute only.
A program may use at most 128 MiB of HBM per device.

```python
import math
import jax
import jax.numpy as jnp
from jax import lax

TILE = 128
K = 64
DEG_MAX = 16
TR_DEV = 32
TILES_DEV = 512
NT = 4096
TILES = 65536
NODES = 524288
N_ROW = 8
N_COL = 16
DEVICES = 128


def draw_row_degree(key, part):
    key = jax.random.fold_in(key, 11)
    key_level, key_full, key_row = jax.random.split(key, 3)
    device_level = jax.random.randint(key_level, (DEVICES,), 1, DEG_MAX // 2 + 1)
    full_device = jax.random.randint(key_full, (), 0, DEVICES)
    owner_device = jnp.arange(NT, dtype=jnp.int32) // TR_DEV
    row_level = device_level[owner_device]
    row_extra = jax.random.randint(key_row, (NT,), 0, DEG_MAX)
    degree = jnp.minimum(row_level + row_extra % (row_level + 1), DEG_MAX)
    return jnp.where(owner_device == full_device, DEG_MAX, degree).astype(jnp.int32)


def draw_tile_column(key, part):
    key = jax.random.fold_in(key, 23)
    key_peer, key_tile = jax.random.split(key, 2)
    slot_index = jnp.arange(TILES, dtype=jnp.int32)
    col_group = slot_index // TILES_DEV % N_COL
    row_peer = jax.random.randint(key_peer, (TILES,), 0, N_ROW)
    local_tile = jax.random.randint(key_tile, (TILES,), 0, TR_DEV)
    return ((row_peer * N_COL + col_group) * TR_DEV + local_tile).astype(jnp.int32)


def draw_node_weight(key, part):
    key = jax.random.fold_in(key, 37)
    position = jnp.arange(NODES, dtype=jnp.float32) / (NODES - 1)
    base_weight = jnp.exp(jax.random.uniform(key, (NODES,), jnp.float32, 0.0, math.log(10.0)))
    return base_weight * 3.0 ** position


def level_of(own_key, extent, cuts, least, top_value):
    gain = 1.0
    for dim, parts in cuts:
        heights = jax.random.uniform(jax.random.fold_in(jax.random.fold_in(own_key, 6), dim), (parts,), jnp.float32, least / len(cuts), top_value / len(cuts))
        gain = gain * jnp.repeat(jnp.exp(heights), extent[dim] // parts).reshape((-1,) + (1,) * (len(extent) - 1 - dim))
    return gain


def noise(own_key, extent, scale, limit, cuts=(), kind=jnp.bfloat16):
    array = jax.random.normal(own_key, extent, jnp.float32) * scale
    if len(cuts) > 0:
        array = level_of(own_key, extent, cuts, -0.22, 0.18) * array
    return jnp.clip(array, min=-limit, max=limit).astype(kind)


def setup_inputs(seed: int = 0) -> dict:
    splits = jax.random.split(jax.random.key(seed), 8)
    return {
        "tile_blocks": noise(splits[0], (TILES, TILE, TILE), (TILE * DEG_MAX // 2) ** -0.5, 0.1875, ((0, 128),)),
        "tile_column": draw_tile_column(jax.random.fold_in(splits[7], 71), 0),
        "row_degree": draw_row_degree(jax.random.fold_in(splits[7], 71), 0),
        "node_weight": draw_node_weight(jax.random.fold_in(splits[7], 71), 0),
        "block_now": noise(splits[4], (NODES, K), 1.0, 6.0, ((0, 128),), jnp.float32),
        "block_prev": noise(splits[5], (NODES, K), 1.0, 6.0, ((0, 128),), jnp.float32),
        "coupling": noise(splits[6], (K, K), K ** -0.5, 0.75, (), jnp.float32),
    }


def row_members(row_degree, slots):
    row_ends = jnp.cumsum(row_degree)
    row_starts = row_ends - row_degree
    position = lax.broadcasted_iota(jnp.int32, (row_degree.shape[0], slots), 1)
    inside = (position >= row_starts[:, None]) & (position < row_ends[:, None])
    return inside.astype(jnp.float32)

def reference(tile_blocks, tile_column, row_degree, node_weight, block_now, block_prev, coupling):
    highest = lax.Precision.HIGHEST
    block_half = block_now.astype(jnp.bfloat16).reshape(NT, TILE, K)

    def one_device(device_index):
        tile_here = lax.dynamic_slice_in_dim(tile_blocks, device_index * TILES_DEV, TILES_DEV, 0)
        columns_here = lax.dynamic_slice_in_dim(tile_column, device_index * TILES_DEV, TILES_DEV, 0)
        degrees = lax.dynamic_slice_in_dim(row_degree, device_index * TR_DEV, TR_DEV, 0)
        picked = block_half[columns_here]
        products = jnp.einsum('sab,sbk->sak', tile_here.astype(jnp.float32), picked.astype(jnp.float32), precision=highest)
        return jnp.einsum('rs,sak->rak', row_members(degrees, TILES_DEV), products, precision=highest)
    spread = lax.map(one_device, jnp.arange(DEVICES, dtype=jnp.int32)).reshape(NODES, K)
    coupled = jnp.dot(block_prev, coupling.T, precision=highest)
    w_raw = node_weight[:, None] * block_now + spread - coupled
    rayleigh = jnp.dot(block_now.T, w_raw, precision=highest) / NODES
    w_next = w_raw - jnp.dot(block_now, rayleigh, precision=highest)
    gram_next = jnp.dot(w_next.T, w_next, precision=highest) / NODES
    lower_factor = jnp.linalg.cholesky(gram_next)
    block_next = jax.scipy.linalg.solve_triangular(lower_factor, w_next.T, lower=True).T
    return (block_next, rayleigh, lower_factor.T)
```

```python
import jax
import jax.numpy as jnp
from jax import lax
from jax.experimental import pallas as pl
from jax.experimental.pallas import tpu as pltpu
from jax.sharding import PartitionSpec as P

TILE = 128
K = 64
ROWS = 32
SLOTS = 512
NODES_DEV = ROWS * TILE
CHAIN = 4
GROUPS = 16
UNROLL = 8
LIST = 576
PARTS = 3
TILES_OF = (64, 128, 64)
WORST = 64.0
F32 = jnp.float32
BF16 = jnp.bfloat16
NT = (((1,), (1,)), ((), ()))
HIGHEST = lax.Precision.HIGHEST


def vmem():
    return pl.BlockSpec(memory_space=pltpu.VMEM)


def smem():
    return pl.BlockSpec(memory_space=pltpu.SMEM)


def params(mib):
    return pltpu.CompilerParams(vmem_limit_bytes=mib << 20)


def split(x):
    hi = x.astype(BF16)
    return hi, (x - hi.astype(F32)).astype(BF16)


def round_kernel(x_ref, half_ref):
    for t in range(ROWS):
        half_ref[t] = x_ref[:, t * TILE:(t + 1) * TILE].astype(BF16)


def build_lists(place_ref, column_ref, degree_ref, list_ref, count_ref):
    z, core = place_ref[0], place_ref[1]

    def one_slot(row):
        def step(slot, ends):
            column = column_ref[slot]
            peer = lax.shift_right_logical(column, 9)
            dz = (lax.shift_right_logical(peer, 1) - z) & 3
            dc = (peer & 1) ^ core
            part = jnp.where(dz == 0, 0, jnp.where(dz == 2, 2, 1))
            tile = (column & 31) + dc * 32 + jnp.where(dz == 1, 64, 0)
            entry = (row << 20) | (slot << 10) | tile
            at = jnp.where(part == 0, ends[0], jnp.where(part == 1, ends[1], ends[2]))
            list_ref[at] = entry
            return tuple(e + jnp.where(part == p, 1, 0) for p, e in enumerate(ends))

        return step

    def one_row(row, carry):
        start, ends = carry
        stop = start + degree_ref[row]
        ends = lax.fori_loop(start, stop, one_slot(row), ends)
        done = []
        for p, e in enumerate(ends):
            @pl.when((e - p * LIST) & 1 == 1)
            def _():
                list_ref[e] = (row << 20) | TILES_OF[p]
            done.append(e + ((e - p * LIST) & 1))
        return stop, tuple(done)

    _, ends = lax.fori_loop(0, ROWS, one_row, (jnp.int32(0), tuple(jnp.int32(p * LIST) for p in range(PARTS))))
    for p, e in enumerate(ends):
        for j in range(2 * UNROLL):
            list_ref[e + j] = TILES_OF[p]
        count_ref[p] = lax.div(e - p * LIST + 2 * UNROLL - 1, 2 * UNROLL)


def multiply_part(part, list_ref, count_ref, tiles_ref, picked_ref, w_ref):
    def group(g, carry):
        base = part * LIST + g * (2 * UNROLL)
        rows, products = [], []
        for u in range(UNROLL):
            first, second = list_ref[base + 2 * u], list_ref[base + 2 * u + 1]
            x = [picked_ref[e & 1023] for e in (first, second)]
            a = [tiles_ref[lax.shift_right_logical(e, 10) & 511] for e in (first, second)]
            rows.append(lax.shift_right_logical(first, 20))
            products.append(lax.dot_general(
                jnp.concatenate(x, axis=1), jnp.concatenate(a, axis=1), NT, preferred_element_type=F32))
        for row, product in zip(rows, products):
            w_ref[row] += product
        return carry

    lax.fori_loop(0, count_ref[part], group, 0)


def place_tiles(picked_ref, blocks):
    at = 0
    for block in blocks:
        n = block.shape[0]
        picked_ref[at:at + n] = block[...]
        at += n
    picked_ref[at] = jnp.zeros((K, TILE), BF16)


def first_kernel(place_ref, column_ref, degree_ref, tiles_ref, half_ref, sib_ref, x_ref, prev_ref, weight_ref,
                 coupling_ref, w_ref, zx_ref, g_ref, list_ref, count_ref, picked_ref):
    build_lists(place_ref, column_ref, degree_ref, list_ref, count_ref)
    chi, clo = split(coupling_ref[...])
    left = jnp.concatenate([chi, chi, clo], axis=1)
    wide = 512
    for c in range(NODES_DEV // wide):
        lanes = slice(c * wide, (c + 1) * wide)
        x = x_ref[:, lanes]
        xhi, xlo = split(x)
        zx_ref[0:K, lanes] = xhi
        zx_ref[K:2 * K, lanes] = xlo
        phi, plo = split(prev_ref[:, lanes])
        coupled = jnp.dot(left, jnp.concatenate([phi, plo, phi], axis=0), preferred_element_type=F32)
        w = x * weight_ref[:, lanes] - coupled
        for t in range(wide // TILE):
            w_ref[c * (wide // TILE) + t] = w[:, t * TILE:(t + 1) * TILE]
    zx = zx_ref[...]
    gg = lax.dot_general(zx[:K], zx, NT, preferred_element_type=F32)
    cross = gg[:, K:]
    g_ref[...] = gg[:, :K] + cross + cross.T
    place_tiles(picked_ref, (half_ref, sib_ref))
    multiply_part(0, list_ref, count_ref, tiles_ref, picked_ref, w_ref)


def second_kernel(list_ref, count_ref, tiles_ref, dn_ref, sdn_ref, up_ref, sup_ref, w_in_ref, w_ref, picked_ref):
    w_ref[...] = w_in_ref[...]
    place_tiles(picked_ref, (dn_ref, sdn_ref, up_ref, sup_ref))
    multiply_part(1, list_ref, count_ref, tiles_ref, picked_ref, w_ref)


def third_kernel(list_ref, count_ref, tiles_ref, f1_ref, f2_ref, s1_ref, s2_ref, w_in_ref, zx_ref, g_ref, zw_ref,
                 sums_ref, w_ref, picked_ref):
    w_ref[...] = w_in_ref[...]
    place_tiles(picked_ref, (f1_ref, f2_ref, s1_ref, s2_ref))
    multiply_part(2, list_ref, count_ref, tiles_ref, picked_ref, w_ref)
    for t in range(ROWS):
        whi, wlo = split(w_ref[t])
        zw_ref[0:K, t * TILE:(t + 1) * TILE] = whi
        zw_ref[K:2 * K, t * TILE:(t + 1) * TILE] = wlo
    zw = zw_ref[...]
    m = lax.dot_general(zx_ref[...], zw, NT, preferred_element_type=F32)
    s = lax.dot_general(zw[:K], zw, NT, preferred_element_type=F32)
    cross = s[:, K:]
    sums_ref[0:K, 0:K] = m[:K, :K] + m[:K, K:] + m[K:, :K]
    sums_ref[0:K, K:] = s[:, :K] + cross + cross.T
    g = g_ref[...]
    sums_ref[K:, 0:K] = g[:K // 2]
    sums_ref[K:, K:] = g[K // 2:]


def factor_kernel(node_total, sums_ref, rayleigh_ref, r_ref, f_ref, flag_ref):
    inv = 1.0 / node_total
    r = sums_ref[0:K, 0:K] * inv
    s = sums_ref[0:K, K:] * inv
    g = jnp.concatenate([sums_ref[K:, 0:K], sums_ref[K:, K:]], axis=0) * inv
    row = lax.broadcasted_iota(jnp.int32, (K, K), 0)
    col = lax.broadcasted_iota(jnp.int32, (K, K), 1)
    eye = jnp.where(row == col, 1.0, 0.0)
    gr = jnp.dot(2.0 * eye - g, r, precision=HIGHEST, preferred_element_type=F32)
    rt = r.T
    gram = s - jnp.dot(rt, gr, precision=HIGHEST, preferred_element_type=F32)
    work = jnp.concatenate([gram, eye], axis=1)
    blocks = [work[8 * b:8 * b + 8] for b in range(K // 8)]
    sub = lax.broadcasted_iota(jnp.int32, (8, 2 * K), 0)
    pivots = []
    for k in range(K):
        b, o = divmod(k, 8)
        line = jnp.broadcast_to(blocks[b][o:o + 1, :], (8, 2 * K))
        pivot = jnp.broadcast_to(blocks[b][o:o + 1, k:k + 1], (8, 2 * K))
        pivots.append(blocks[b][o:o + 1, k:k + 1])
        scaled = line / pivot
        for i in range(b, K // 8):
            column = jnp.broadcast_to(blocks[i][:, k:k + 1], (8, 2 * K))
            if i == b:
                column = jnp.where(sub > o, column, 0.0)
            blocks[i] = blocks[i] - column * scaled
    pivot = jnp.concatenate(pivots, axis=0)
    work = jnp.concatenate(blocks, axis=0) * lax.rsqrt(pivot)
    upper = jnp.where(col >= row, work[:, :K], 0.0)
    lower_inv = jnp.where(col <= row, work[:, K:], 0.0)
    rayleigh_ref[...] = r
    r_ref[...] = upper
    f_ref[:, 0:K] = lower_inv
    f_ref[:, K:] = -jnp.dot(lower_inv, rt, precision=HIGHEST, preferred_element_type=F32)
    largest = jnp.max(jnp.where(row == col, s, 0.0))
    smallest = jnp.min(pivot)
    flag_ref[0] = jnp.where(smallest * WORST >= largest, 0, 1).astype(jnp.int32)


def final_kernel(f_ref, zw_ref, zx_ref, out_ref):
    f1h, f1l = split(f_ref[:, 0:K])
    f2h, f2l = split(f_ref[:, K:])
    zero = jnp.zeros((K, K), BF16)
    left = jnp.concatenate([jnp.concatenate([f1h, f1h, f2h, f2h], axis=1),
                            jnp.concatenate([f1l, zero, f2l, zero], axis=1)], axis=0)
    wide = 512
    for c in range(NODES_DEV // wide):
        lanes = slice(c * wide, (c + 1) * wide)
        z = jnp.concatenate([zw_ref[:, lanes], zx_ref[:, lanes]], axis=0)
        y = jnp.dot(left, z, preferred_element_type=F32)
        out_ref[:, lanes] = y[:K] + y[K:]


def exchange(v, axis, to):
    n = lax.axis_size(axis)
    return lax.ppermute(v, axis, [(i, to(i)) for i in range(n)])


def core_swap(v):
    return exchange(v, "row", lambda i: i ^ 1)


def along_z(v, d):
    return exchange(v, "row", lambda i: (i + 2 * d) % 8)


def total(v):
    v = v + core_swap(v)
    for axis, unit in (("row", 2), ("col", 1), ("col", 4)):
        others = [exchange(v, axis, lambda i, d=d * unit: i ^ d) for d in (1, 2, 3)]
        v = (v + others[0]) + (others[1] + others[2])
    return v


def local(tile_blocks, tile_column, row_degree, node_weight, block_now, block_prev, coupling):
    node_total = NODES_DEV * lax.axis_size("row") * lax.axis_size("col")
    x = block_now.T
    prev = block_prev.T
    row = lax.axis_index("row")
    place = jnp.stack([row // 2, row % 2]).astype(jnp.int32)
    tiles = pltpu.with_memory_space_constraint(tile_blocks, pltpu.VMEM)
    slab = (ROWS, K, TILE)
    half = pl.pallas_call(
        round_kernel, out_shape=jax.ShapeDtypeStruct(slab, BF16), in_specs=[vmem()], out_specs=vmem(),
        compiler_params=params(8), name="round_block")(x)
    sib = core_swap(half)
    dn = along_z(half, 1)
    up = along_z(half, -1)

    w1, zx, g, lists, counts = pl.pallas_call(
        first_kernel,
        out_shape=(pltpu.VMEM(slab, F32), pltpu.VMEM((2 * K, NODES_DEV), BF16), pltpu.VMEM((K, K), F32),
                   pltpu.SMEM((PARTS * LIST + 64,), jnp.int32), pltpu.SMEM((PARTS,), jnp.int32)),
        in_specs=[smem(), smem(), smem()] + [vmem()] * 7,
        out_specs=(vmem(), vmem(), vmem(), smem(), smem()),
        scratch_shapes=[pltpu.VMEM((TILES_OF[0] + 1, K, TILE), BF16)],
        compiler_params=params(12), name="own_part")(
            place, tile_column, row_degree, tiles, half, sib, x, prev, node_weight.reshape(1, NODES_DEV), coupling)

    h = ROWS // 2
    f1 = along_z(dn[:h], 1)
    f2 = along_z(up[h:], -1)
    sdn = core_swap(dn)
    sup = core_swap(up)
    w2 = pl.pallas_call(
        second_kernel, out_shape=pltpu.VMEM(slab, F32),
        in_specs=[smem(), smem()] + [vmem()] * 6, out_specs=vmem(),
        scratch_shapes=[pltpu.VMEM((TILES_OF[1] + 1, K, TILE), BF16)],
        compiler_params=params(12), name="near_part")(lists, counts, tiles, dn, sdn, up, sup, w1)

    s1 = core_swap(f1)
    s2 = core_swap(f2)
    zw, sums = pl.pallas_call(
        third_kernel,
        out_shape=(pltpu.VMEM((2 * K, NODES_DEV), BF16), jax.ShapeDtypeStruct((K + K // 2, 2 * K), F32)),
        in_specs=[smem(), smem()] + [vmem()] * 8, out_specs=(vmem(), vmem()),
        scratch_shapes=[pltpu.VMEM(slab, F32), pltpu.VMEM((TILES_OF[2] + 1, K, TILE), BF16)],
        compiler_params=params(16), name="far_part")(lists, counts, tiles, f1, f2, s1, s2, w2, zx, g)

    sums = total(sums)
    square = jax.ShapeDtypeStruct((K, K), F32)
    rayleigh, r_factor, f, flag = pl.pallas_call(
        lambda *refs: factor_kernel(node_total, *refs),
        out_shape=(square, square, jax.ShapeDtypeStruct((K, 2 * K), F32), jax.ShapeDtypeStruct((1,), jnp.int32)),
        in_specs=[vmem()], out_specs=(vmem(), vmem(), vmem(), smem()),
        compiler_params=params(8), name="factor")(sums)

    def plain(zw, zx, f, rayleigh, r_factor):
        out = pl.pallas_call(
            final_kernel, out_shape=jax.ShapeDtypeStruct((K, NODES_DEV), F32), in_specs=[vmem()] * 3,
            out_specs=vmem(), compiler_params=params(12), name="scale_block")(f, zw, zx)
        return out, r_factor

    def two_passes(zw, zx, f, rayleigh, r_factor):
        whole = lambda z: z[:K].astype(F32) + z[K:].astype(F32)
        w_next = whole(zw) - jnp.dot(rayleigh.T, whole(zx), precision=HIGHEST)
        gram = total(jnp.dot(w_next, w_next.T, precision=HIGHEST)) / node_total
        lower = jnp.linalg.cholesky(gram)
        return jax.scipy.linalg.solve_triangular(lower, w_next, lower=True), lower.T

    out, r_factor = lax.cond(flag[0] == 0, plain, two_passes, zw, zx, f, rayleigh, r_factor)
    return out.T, rayleigh, r_factor


def solution(mesh):
    in_specs = (
        P(("row", "col"), None, None),
        P(("row", "col")),
        P(("row", "col")),
        P(("row", "col")),
        P(("row", "col"), None),
        P(("row", "col"), None),
        P(),
    )
    out_specs = (P(("row", "col"), None), P(), P())
    return jax.shard_map(local, mesh=mesh, in_specs=in_specs, out_specs=out_specs, check_vma=False)
```

```python
import functools
import jax
import jax.numpy as jnp
from jax import lax
from jax.experimental import pallas as pl
from jax.experimental.pallas import tpu as pltpu
from jax.sharding import PartitionSpec as P

TILE = 128
K = 64
ROWS = 32
SLOTS = 512
NODES_DEV = ROWS * TILE
UNROLL = 8
LIST = 576
PARTS = 4
PART_TILES = 64
CHUNKS = 8
WORST = 32.0
F32 = jnp.float32
BF16 = jnp.bfloat16
NT = (((1,), (1,)), ((), ()))
HIGHEST = lax.Precision.HIGHEST
SLAB = (ROWS, K, TILE)


def vmem():
    return pl.BlockSpec(memory_space=pltpu.VMEM)


def smem():
    return pl.BlockSpec(memory_space=pltpu.SMEM)


def hbm():
    return pl.BlockSpec(memory_space=pltpu.HBM)


def in_hbm(x):
    return pltpu.with_memory_space_constraint(x, pltpu.HBM)


def call(kernel, name, out_shape, in_specs, out_specs, mib, us, scratch=()):
    return pl.pallas_call(
        kernel, out_shape=out_shape, in_specs=in_specs, out_specs=out_specs, scratch_shapes=list(scratch), name=name,
        compiler_params=pltpu.CompilerParams(vmem_limit_bytes=mib << 20),
        cost_estimate=pl.CostEstimate(flops=int(us * 1e9), bytes_accessed=int(us * 3e6), transcendentals=0))


def split(x):
    hi = x.astype(BF16)
    return hi, (x - hi.astype(F32)).astype(BF16)


def dot3(a, b):
    ah, al = split(a)
    bh, bl = split(b)
    return jnp.dot(jnp.concatenate([ah, ah, al], axis=1), jnp.concatenate([bh, bl, bh], axis=0),
                   preferred_element_type=F32)


def round_kernel(x_hbm, half_ref, x_ref, sems):
    wide = NODES_DEV // 4
    copies = [pltpu.make_async_copy(x_hbm.at[:, c * wide:(c + 1) * wide], x_ref.at[:, c * wide:(c + 1) * wide],
                                    sems.at[c]) for c in range(4)]
    for copy in copies:
        copy.start()
    for c, copy in enumerate(copies):
        copy.wait()
        for t in range(c * wide // TILE, (c + 1) * wide // TILE):
            half_ref[t] = x_ref[:, t * TILE:(t + 1) * TILE].astype(BF16)


def build_lists(column, degree, table_ref, count_ref):
    member_row = lax.axis_index("row")
    z = lax.shift_right_logical(member_row, 1)
    core = member_row & 1
    from_z = (z + 3 + 2 * core) & 3
    peer = lax.shift_right_logical(column, 9)
    peer_z = lax.shift_right_logical(peer, 1)
    dz = (peer_z - z) & 3
    dc = (peer & 1) ^ core
    side = jnp.where(peer_z == from_z, 1, 0)
    odd = (dz & 1) == 1
    part = jnp.where(odd, jnp.where(side == 1 - dc, 1, 2), jnp.where(dz == 0, 0, 3))
    tile = (column & 31) + 32 * jnp.where(odd, 1 - side, dc)
    r_i = lax.broadcasted_iota(jnp.int32, (ROWS, ROWS), 0)
    r_j = lax.broadcasted_iota(jnp.int32, (ROWS, ROWS), 1)
    degrees = jnp.broadcast_to(degree, (ROWS, ROWS))
    starts = jnp.sum(jnp.where(r_j < r_i, degrees, 0), axis=1, keepdims=True)
    ends = jnp.sum(jnp.where(r_j <= r_i, degrees, 0), axis=1, keepdims=True)
    s = lax.broadcasted_iota(jnp.int32, (ROWS, SLOTS), 1)
    member = jnp.where((s >= starts) & (s < ends), 1.0, 0.0)
    row = jnp.sum(member * lax.broadcasted_iota(jnp.int32, (ROWS, SLOTS), 0).astype(F32), axis=0, keepdims=True)
    used = jnp.sum(member, axis=0, keepdims=True)
    member = member.astype(BF16)
    line = lax.broadcasted_iota(jnp.int32, (8, SLOTS), 0)
    mine = jnp.where((line == part) & (used > 0.5), 1.0, 0.0)
    mine_half = mine.astype(BF16)
    s_i = lax.broadcasted_iota(jnp.int32, (SLOTS, SLOTS), 0)
    s_j = lax.broadcasted_iota(jnp.int32, (SLOTS, SLOTS), 1)
    before = jnp.where(s_i < s_j, 1.0, 0.0).astype(BF16)
    rank = jnp.dot(mine_half, before, preferred_element_type=F32)
    per_row = lax.dot_general(mine_half, member, NT, preferred_element_type=F32).astype(jnp.int32)
    pad = per_row & 1
    earlier = jnp.where(r_i < r_j, 1.0, 0.0).astype(BF16)
    pads = jnp.dot(pad.astype(F32).astype(BF16), earlier, preferred_element_type=F32)
    shift = jnp.dot(pads.astype(BF16), member, preferred_element_type=F32)
    base = (line * LIST).astype(F32)
    place = (jnp.sum(mine * (rank + shift + base + 1.0), axis=0, keepdims=True) - 1.0).astype(jnp.int32)
    slot = lax.broadcasted_iota(jnp.int32, (1, SLOTS), 1)
    values = jnp.where(line == 0, tile, jnp.where(line == 1, slot & 31, jnp.where(
        line == 2, lax.shift_right_logical(slot, 5), jnp.where(line == 3, row.astype(jnp.int32), 1))))
    values = values.astype(F32).astype(BF16)
    for c in range(PARTS * LIST // 256):
        at = lax.broadcasted_iota(jnp.int32, (256, SLOTS), 0) + c * 256
        hot = jnp.where(at == place, 1.0, 0.0).astype(BF16)
        got = lax.dot_general(values, hot, NT, preferred_element_type=F32).astype(jnp.int32)
        entry = got[0:1] | (got[1:2] << 10) | (got[2:3] << 15) | (got[3:4] << 20)
        table_ref[0:1, c * 256:(c + 1) * 256] = jnp.where(got[4:5] > 0, entry, PART_TILES)
    length = jnp.sum(per_row + pad, axis=1, keepdims=True)
    first = lax.broadcasted_iota(jnp.int32, (8, 1), 0)
    for p in range(PARTS):
        n = jnp.sum(jnp.where(first == p, length, 0))
        count_ref[p] = lax.div(n + 2 * UNROLL - 1, 2 * UNROLL)


def multiply_part(part, list_ref, count_ref, tiles_ref, picked_ref, w_ref):
    def group(g, carry):
        base = part * LIST + g * (2 * UNROLL)
        rows, products = [], []
        for u in range(UNROLL):
            first, second = list_ref[0, base + 2 * u], list_ref[0, base + 2 * u + 1]
            x = [picked_ref[e & 127] for e in (first, second)]
            a = [tiles_ref[lax.shift_right_logical(e, 10) & 511] for e in (first, second)]
            rows.append(lax.shift_right_logical(first, 20))
            products.append(lax.dot_general(
                jnp.concatenate(x, axis=1), jnp.concatenate(a, axis=1), NT, preferred_element_type=F32))
        for row, product in zip(rows, products):
            w_ref[row] += product
        return carry

    lax.fori_loop(0, count_ref[part], group, 0)


def place_tiles(picked_ref, first_ref, second_ref):
    picked_ref[0:ROWS] = first_ref[...]
    picked_ref[ROWS:2 * ROWS] = second_ref[...]
    picked_ref[PART_TILES] = jnp.zeros((K, TILE), BF16)


def prepare_kernel(tiles_hbm, column_hbm, degree_hbm, prev_hbm, weight_hbm, coupling_hbm, x_ref,
                   tiles_ref, w_ref, zx_ref, g_ref, list_ref, count_ref,
                   column_ref, degree_ref, prev_ref, weight_ref, coupling_ref, table_ref, sems, tile_sems):
    small = [pltpu.make_async_copy(a, b, sems.at[i]) for i, (a, b) in enumerate((
        (column_hbm, column_ref), (degree_hbm, degree_ref), (coupling_hbm, coupling_ref), (weight_hbm, weight_ref),
        (prev_hbm, prev_ref)))]
    n = SLOTS // CHUNKS
    large = [pltpu.make_async_copy(tiles_hbm.at[c * n:(c + 1) * n], tiles_ref.at[c * n:(c + 1) * n], tile_sems.at[c])
             for c in range(CHUNKS)]
    for copy in small + large:
        copy.start()
    small[0].wait()
    small[1].wait()
    build_lists(column_ref[...], degree_ref[...], table_ref, count_ref)
    table = pltpu.make_async_copy(table_ref, list_ref, sems.at[5])
    table.start()
    for copy in small[2:]:
        copy.wait()
    chi, clo = split(coupling_ref[...])
    left = jnp.concatenate([chi, chi, clo], axis=1)
    wide = 512
    for c in range(NODES_DEV // wide):
        lanes = slice(c * wide, (c + 1) * wide)
        x = x_ref[:, lanes]
        xhi, xlo = split(x)
        zx_ref[0:K, lanes] = xhi
        zx_ref[K:2 * K, lanes] = xlo
        phi, plo = split(prev_ref[:, lanes])
        coupled = jnp.dot(left, jnp.concatenate([phi, plo, phi], axis=0), preferred_element_type=F32)
        w = x * weight_ref[:, lanes] - coupled
        for t in range(wide // TILE):
            w_ref[c * (wide // TILE) + t] = w[:, t * TILE:(t + 1) * TILE]
    zx = zx_ref[...]
    gg = lax.dot_general(zx[:K], zx, NT, preferred_element_type=F32)
    cross = gg[:, K:]
    g_ref[...] = gg[:, :K] + cross + cross.T
    table.wait()
    for copy in large:
        copy.wait()


def near_kernel(list_ref, count_ref, tiles_ref, half_ref, sib_ref, a_ref, b_ref, w_in_ref, w_ref, picked_ref):
    w_ref[...] = w_in_ref[...]
    place_tiles(picked_ref, half_ref, sib_ref)
    multiply_part(0, list_ref, count_ref, tiles_ref, picked_ref, w_ref)
    place_tiles(picked_ref, a_ref, b_ref)
    multiply_part(1, list_ref, count_ref, tiles_ref, picked_ref, w_ref)


def middle_kernel(list_ref, count_ref, tiles_ref, a_ref, b_ref, w_in_ref, w_ref, picked_ref):
    w_ref[...] = w_in_ref[...]
    place_tiles(picked_ref, a_ref, b_ref)
    multiply_part(2, list_ref, count_ref, tiles_ref, picked_ref, w_ref)


def far_kernel(list_ref, count_ref, tiles_ref, a_ref, b_ref, w_in_ref, zx_ref, g_ref, zw_ref, sums_ref, w_ref,
               picked_ref):
    w_ref[...] = w_in_ref[...]
    place_tiles(picked_ref, a_ref, b_ref)
    multiply_part(3, list_ref, count_ref, tiles_ref, picked_ref, w_ref)
    for t in range(ROWS):
        whi, wlo = split(w_ref[t])
        zw_ref[0:K, t * TILE:(t + 1) * TILE] = whi
        zw_ref[K:2 * K, t * TILE:(t + 1) * TILE] = wlo
    zw = zw_ref[...]
    m = lax.dot_general(zx_ref[...], zw, NT, preferred_element_type=F32)
    s = lax.dot_general(zw[:K], zw, NT, preferred_element_type=F32)
    cross = s[:, K:]
    sums_ref[0:K, 0:K] = m[:K, :K] + m[:K, K:] + m[K:, :K]
    sums_ref[0:K, K:] = s[:, :K] + cross + cross.T
    g = g_ref[...]
    sums_ref[K:, 0:K] = g[:K // 2]
    sums_ref[K:, K:] = g[K // 2:]


def eliminate(blocks):
    shape = blocks[0].shape
    count = len(blocks)
    sub = lax.broadcasted_iota(jnp.int32, shape, 0)
    wide = lambda v: jnp.broadcast_to(v, shape)
    done, pivots = [None] * count, []
    for start in range(0, 8 * count, 4):
        b, o = divmod(start, 8)
        head = blocks[b]
        line = [wide(head[o + j:o + j + 1, :]) for j in range(4)]
        column = [[wide(blocks[i][:, start + j:start + j + 1]) for j in range(4)] for i in range(b, count)]
        a = [[wide(column[0][l][o + j:o + j + 1, :]) for l in range(4)] for j in range(4)]
        inverse, m = [None] * 4, {}
        for j in range(4):
            inverse[j] = 1.0 / a[j][j]
            for t in range(j + 1, 4):
                m[t, j] = a[j][t] * inverse[j]
                for l in range(t, 4):
                    a[t][l] = a[t][l] - m[t, j] * a[j][l]
            for t in range(j + 1, 4):
                line[t] = line[t] - m[t, j] * line[j]
        scaled = [line[j] * inverse[j] for j in range(4)]
        for i in range(b, count):
            if i == b and o == 4:
                continue
            c = column[i - b]
            for j in range(4):
                for t in range(j + 1, 4):
                    c[t] = c[t] - m[t, j] * c[j]
            blocks[i] = blocks[i] - ((c[0] * scaled[0] + c[1] * scaled[1]) + (c[2] * scaled[2] + c[3] * scaled[3]))
        rows = blocks[b] if done[b] is None else done[b]
        for j in range(4):
            rows = jnp.where(sub == o + j, line[j] * lax.rsqrt(a[j][j]), rows)
            pivots.append(a[j][j])
        done[b] = rows
    return done, pivots


def factor_kernel(node_total, sums_ref, rayleigh_ref, r_ref, f_ref, flag_ref):
    inv = 1.0 / node_total
    r = sums_ref[0:K, 0:K] * inv
    s = sums_ref[0:K, K:] * inv
    g = jnp.concatenate([sums_ref[K:, 0:K], sums_ref[K:, K:]], axis=0) * inv
    row = lax.broadcasted_iota(jnp.int32, (K, K), 0)
    col = lax.broadcasted_iota(jnp.int32, (K, K), 1)
    eye = jnp.where(row == col, 1.0, 0.0)
    rt = r.T
    gram = s - dot3(rt, dot3(2.0 * eye - g, r))
    work = jnp.concatenate([gram, eye], axis=1)
    done, pivots = eliminate([work[8 * b:8 * b + 8] for b in range(K // 8)])
    work = jnp.concatenate(done, axis=0)
    lower_inv = jnp.where(col <= row, work[:, K:], 0.0)
    rayleigh_ref[...] = r
    r_ref[...] = jnp.where(col >= row, work[:, :K], 0.0)
    f_ref[:, 0:K] = lower_inv
    f_ref[:, K:] = -dot3(lower_inv, rt)
    largest = jnp.max(jnp.where(row == col, s, 0.0))
    smallest = jnp.min(functools.reduce(jnp.minimum, pivots))
    flag_ref[0] = jnp.where(smallest * WORST >= largest, 0, 1).astype(jnp.int32)


def final_kernel(f_ref, zw_ref, zx_ref, out_ref):
    f1h, f1l = split(f_ref[:, 0:K])
    f2h, f2l = split(f_ref[:, K:])
    zero = jnp.zeros((K, K), BF16)
    left = jnp.concatenate([jnp.concatenate([f1h, f1h, f2h, f2h], axis=1),
                            jnp.concatenate([f1l, zero, f2l, zero], axis=1)], axis=0)
    wide = 512
    for c in range(NODES_DEV // wide):
        lanes = slice(c * wide, (c + 1) * wide)
        z = jnp.concatenate([zw_ref[:, lanes], zx_ref[:, lanes]], axis=0)
        y = jnp.dot(left, z, preferred_element_type=F32)
        out_ref[:, lanes] = y[:K] + y[K:]


def exchange(v, axis, to):
    n = lax.axis_size(axis)
    return lax.ppermute(v, axis, [(i, to(i)) for i in range(n)])


def core_swap(v):
    return exchange(v, "row", lambda i: i ^ 1)


def onward(v):
    return exchange(v, "row", lambda i: (i + (2 if i % 2 == 0 else 6)) % 8)


def total(v):
    v = v + core_swap(v)
    for axis, unit in (("row", 2), ("col", 1), ("col", 4)):
        others = [exchange(v, axis, lambda i, d=d * unit: i ^ d) for d in (1, 2, 3)]
        v = (v + others[0]) + (others[1] + others[2])
    return v


def local(tile_blocks, tile_column, row_degree, node_weight, block_now, block_prev, coupling):
    node_total = NODES_DEV * lax.axis_size("row") * lax.axis_size("col")
    after = lax.optimization_barrier
    slab_vmem = pltpu.VMEM(SLAB, F32)
    picked = pltpu.VMEM((PART_TILES + 1, K, TILE), BF16)
    pair_vmem = pltpu.VMEM((2 * K, NODES_DEV), BF16)
    square = jax.ShapeDtypeStruct((K, K), F32)

    half, x = call(
        round_kernel, "round_block", (pltpu.VMEM(SLAB, BF16), pltpu.VMEM((K, NODES_DEV), F32)), [hbm()],
        (vmem(), vmem()), 8, 1, [pltpu.SemaphoreType.DMA((4,))])(in_hbm(block_now.T))
    a1 = onward(half)
    sib = core_swap(half)
    sib, x = after((sib, x))
    a2 = onward(sib)
    tiles, w1, zx, g, lists, counts = call(
        prepare_kernel, "prepare",
        (pltpu.VMEM((SLOTS, TILE, TILE), BF16), slab_vmem, pair_vmem, pltpu.VMEM((K, K), F32),
         pltpu.SMEM((1, PARTS * LIST), jnp.int32), pltpu.SMEM((PARTS,), jnp.int32)),
        [hbm()] * 6 + [vmem()], (vmem(), vmem(), vmem(), vmem(), smem(), smem()), 16, 7,
        [pltpu.VMEM((1, SLOTS), jnp.int32), pltpu.VMEM((1, ROWS), jnp.int32), pltpu.VMEM((K, NODES_DEV), F32),
         pltpu.VMEM((1, NODES_DEV), F32), pltpu.VMEM((K, K), F32), pltpu.VMEM((1, PARTS * LIST), jnp.int32),
         pltpu.SemaphoreType.DMA((6,)), pltpu.SemaphoreType.DMA((CHUNKS,))])(
            in_hbm(tile_blocks), in_hbm(tile_column.reshape(1, SLOTS)), in_hbm(row_degree.reshape(1, ROWS)),
            in_hbm(block_prev.T), in_hbm(node_weight.reshape(1, NODES_DEV)), in_hbm(coupling), x)

    a1, w1 = after((a1, w1))
    a3 = onward(a1)
    b1 = core_swap(a1)
    w2 = call(near_kernel, "near_parts", slab_vmem, [smem(), smem()] + [vmem()] * 6, vmem(), 12, 5, [picked])(
        lists, counts, tiles, half, sib, a1, b1, w1)
    a2, w2 = after((a2, w2))
    b2 = core_swap(a2)
    w3 = call(middle_kernel, "middle_part", slab_vmem, [smem(), smem()] + [vmem()] * 4, vmem(), 12, 3, [picked])(
        lists, counts, tiles, a2, b2, w2)
    a3, w3 = after((a3, w3))
    b3 = core_swap(a3)
    zw, sums = call(
        far_kernel, "far_part", (pair_vmem, jax.ShapeDtypeStruct((K + K // 2, 2 * K), F32)),
        [smem(), smem()] + [vmem()] * 6, (vmem(), vmem()), 16, 5, [slab_vmem, picked])(
            lists, counts, tiles, a3, b3, w3, zx, g)

    sums = total(sums)
    rayleigh, r_factor, f, flag = call(
        functools.partial(factor_kernel, node_total), "factor",
        (square, square, jax.ShapeDtypeStruct((K, 2 * K), F32), jax.ShapeDtypeStruct((1,), jnp.int32)),
        [vmem()], (vmem(), vmem(), vmem(), smem()), 8, 5)(sums)

    def plain(zw, zx, f, sums, r_factor):
        out = call(final_kernel, "scale_block", jax.ShapeDtypeStruct((K, NODES_DEV), F32), [vmem()] * 3, vmem(), 12, 2)(
            f, zw, zx)
        return out, r_factor

    def two_passes(zw, zx, f, sums, r_factor):
        whole = lambda z: z[:K].astype(F32) + z[K:].astype(F32)
        rayleigh_t = sums[:K, :K].T / node_total
        w_next = whole(zw) - jnp.dot(rayleigh_t, whole(zx), precision=HIGHEST)
        gram = total(jnp.dot(w_next, w_next.T, precision=HIGHEST)) / node_total
        lower = jnp.linalg.cholesky(gram)
        return jax.scipy.linalg.solve_triangular(lower, w_next, lower=True), lower.T

    out, r_factor = lax.cond(flag[0] == 0, plain, two_passes, zw, zx, f, sums, r_factor)
    return out.T, rayleigh, r_factor


def solution(mesh):
    in_specs = (
        P(("row", "col"), None, None),
        P(("row", "col")),
        P(("row", "col")),
        P(("row", "col")),
        P(("row", "col"), None),
        P(("row", "col"), None),
        P(),
    )
    out_specs = (P(("row", "col"), None), P(), P())
    return jax.shard_map(local, mesh=mesh, in_specs=in_specs, out_specs=out_specs, check_vma=False)
```

```python
import functools
import jax
import jax.numpy as jnp
from jax import lax
from jax.experimental import pallas as pl
from jax.experimental.pallas import tpu as pltpu
from jax.sharding import PartitionSpec as P

TILE = 128
K = 64
ROWS = 32
SLOTS = 512
NODES_DEV = ROWS * TILE
UNROLL = 8
LIST = 576
PARTS = 4
CHUNKS = 8
WORST = 32.0
F32 = jnp.float32
BF16 = jnp.bfloat16
NT = (((1,), (1,)), ((), ()))
HIGHEST = lax.Precision.HIGHEST
SLAB = (ROWS, K, TILE)


def vmem():
    return pl.BlockSpec(memory_space=pltpu.VMEM)


def smem():
    return pl.BlockSpec(memory_space=pltpu.SMEM)


def hbm():
    return pl.BlockSpec(memory_space=pltpu.HBM)


def in_hbm(x):
    return pltpu.with_memory_space_constraint(x, pltpu.HBM)


def call(kernel, name, out_shape, in_specs, out_specs, mib, us, scratch=(), aliases=None):
    return pl.pallas_call(
        kernel, out_shape=out_shape, in_specs=in_specs, out_specs=out_specs, scratch_shapes=list(scratch), name=name,
        input_output_aliases=aliases or {},
        compiler_params=pltpu.CompilerParams(vmem_limit_bytes=mib << 20),
        cost_estimate=pl.CostEstimate(flops=int(us * 1e5), bytes_accessed=int(us * 1e3), transcendentals=0))


def split(x):
    hi = x.astype(BF16)
    return hi, (x - hi.astype(F32)).astype(BF16)


def dot3(a, b):
    ah, al = split(a)
    bh, bl = split(b)
    return jnp.dot(jnp.concatenate([ah, ah, al], axis=1), jnp.concatenate([bh, bl, bh], axis=0),
                   preferred_element_type=F32)


def round_kernel(x_hbm, half_ref, x_ref, sems):
    wide = NODES_DEV // 4
    copies = [pltpu.make_async_copy(x_hbm.at[:, c * wide:(c + 1) * wide], x_ref.at[:, c * wide:(c + 1) * wide],
                                    sems.at[c]) for c in range(4)]
    for copy in copies:
        copy.start()
    for c, copy in enumerate(copies):
        copy.wait()
        for t in range(c * wide // TILE, (c + 1) * wide // TILE):
            half_ref[t] = x_ref[:, t * TILE:(t + 1) * TILE].astype(BF16)


def build_lists(column, degree, table_ref, count_ref):
    member_row = lax.axis_index("row")
    z = lax.shift_right_logical(member_row, 1)
    core = member_row & 1
    from_z = (z + 3 + 2 * core) & 3
    peer = lax.shift_right_logical(column, 9)
    peer_z = lax.shift_right_logical(peer, 1)
    dz = (peer_z - z) & 3
    dc = (peer & 1) ^ core
    side = jnp.where(peer_z == from_z, 1, 0)
    odd = (dz & 1) == 1
    late = odd & (side == dc)
    far = dz == 2
    part = jnp.where(far, 2 + dc, jnp.where(late, 1, 0))
    tile = 1 + (column & 31) + jnp.where(far, 0, 32 * dc) + jnp.where(odd & (side != dc), 64, 0)
    r_i = lax.broadcasted_iota(jnp.int32, (ROWS, ROWS), 0)
    r_j = lax.broadcasted_iota(jnp.int32, (ROWS, ROWS), 1)
    degrees = jnp.broadcast_to(degree, (ROWS, ROWS))
    starts = jnp.sum(jnp.where(r_j < r_i, degrees, 0), axis=1, keepdims=True)
    ends = jnp.sum(jnp.where(r_j <= r_i, degrees, 0), axis=1, keepdims=True)
    s = lax.broadcasted_iota(jnp.int32, (ROWS, SLOTS), 1)
    member = jnp.where((s >= starts) & (s < ends), 1.0, 0.0)
    row = jnp.sum(member * lax.broadcasted_iota(jnp.int32, (ROWS, SLOTS), 0).astype(F32), axis=0, keepdims=True)
    used = jnp.sum(member, axis=0, keepdims=True)
    member = member.astype(BF16)
    line = lax.broadcasted_iota(jnp.int32, (8, SLOTS), 0)
    mine = jnp.where((line == part) & (used > 0.5), 1.0, 0.0)
    mine_half = mine.astype(BF16)
    s_i = lax.broadcasted_iota(jnp.int32, (SLOTS, SLOTS), 0)
    s_j = lax.broadcasted_iota(jnp.int32, (SLOTS, SLOTS), 1)
    before = jnp.where(s_i < s_j, 1.0, 0.0).astype(BF16)
    rank = jnp.dot(mine_half, before, preferred_element_type=F32)
    per_row = lax.dot_general(mine_half, member, NT, preferred_element_type=F32).astype(jnp.int32)
    pad = per_row & 1
    earlier = jnp.where(r_i < r_j, 1.0, 0.0).astype(BF16)
    pads = jnp.dot(pad.astype(F32).astype(BF16), earlier, preferred_element_type=F32)
    shift = jnp.dot(pads.astype(BF16), member, preferred_element_type=F32)
    base = (line * LIST).astype(F32)
    place = (jnp.sum(mine * (rank + shift + base + 1.0), axis=0, keepdims=True) - 1.0).astype(jnp.int32)
    slot = lax.broadcasted_iota(jnp.int32, (1, SLOTS), 1)
    values = jnp.where(line == 0, tile, jnp.where(line == 1, slot & 31, jnp.where(
        line == 2, lax.shift_right_logical(slot, 5), row.astype(jnp.int32))))
    values = values.astype(F32).astype(BF16)
    for c in range(PARTS * LIST // 256):
        at = lax.broadcasted_iota(jnp.int32, (256, SLOTS), 0) + c * 256
        hot = jnp.where(at == place, 1.0, 0.0).astype(BF16)
        got = lax.dot_general(values, hot, NT, preferred_element_type=F32).astype(jnp.int32)
        table_ref[0:1, c * 256:(c + 1) * 256] = got[0:1] | (got[1:2] << 10) | (got[2:3] << 15) | (got[3:4] << 20)
    length = jnp.sum(per_row + pad, axis=1, keepdims=True)
    first = lax.broadcasted_iota(jnp.int32, (8, 1), 0)
    for p in range(PARTS):
        n = jnp.sum(jnp.where(first == p, length, 0))
        count_ref[p] = lax.div(n + 2 * UNROLL - 1, 2 * UNROLL)


def multiply_part(part, list_ref, count_ref, tiles_ref, picked_ref, w_ref):
    def group(g, carry):
        base = part * LIST + g * (2 * UNROLL)
        rows, products = [], []
        for u in range(UNROLL):
            first, second = list_ref[0, base + 2 * u], list_ref[0, base + 2 * u + 1]
            x = [picked_ref[e & 255] for e in (first, second)]
            a = [tiles_ref[lax.shift_right_logical(e, 10) & 511] for e in (first, second)]
            rows.append(lax.shift_right_logical(first, 20))
            products.append(lax.dot_general(
                jnp.concatenate(x, axis=1), jnp.concatenate(a, axis=1), NT, preferred_element_type=F32))
        for row, product in zip(rows, products):
            w_ref[row] += product
        return carry

    lax.fori_loop(0, count_ref[part], group, 0)


def place_tiles(picked_ref, *blocks):
    picked_ref[0] = jnp.zeros((K, TILE), BF16)
    at = 1
    for block in blocks:
        picked_ref[at:at + block.shape[0]] = block[...]
        at += block.shape[0]


def tile_copies(tiles_hbm, tiles_ref, sems):
    n = SLOTS // CHUNKS
    spans = [slice(c * n, (c + 1) * n) for c in range(CHUNKS)]
    return [pltpu.make_async_copy(tiles_hbm.at[span], tiles_ref.at[span], sems.at[c]) for c, span in enumerate(spans)]


def prepare_kernel(tiles_hbm, column_hbm, degree_hbm, prev_hbm, weight_hbm, coupling_hbm, x_ref,
                   tiles_ref, w_ref, zx_ref, g_ref, list_ref, count_ref,
                   column_ref, degree_ref, prev_ref, weight_ref, coupling_ref, table_ref, sems, tile_sems):
    small = [pltpu.make_async_copy(a, b, sems.at[i]) for i, (a, b) in enumerate((
        (column_hbm, column_ref), (degree_hbm, degree_ref), (coupling_hbm, coupling_ref), (weight_hbm, weight_ref),
        (prev_hbm, prev_ref)))]
    large = tile_copies(tiles_hbm, tiles_ref, tile_sems)
    for copy in small + large:
        copy.start()
    small[0].wait()
    small[1].wait()
    build_lists(column_ref[...], degree_ref[...], table_ref, count_ref)
    table = pltpu.make_async_copy(table_ref, list_ref, sems.at[5])
    table.start()
    for copy in small[2:]:
        copy.wait()
    chi, clo = split(coupling_ref[...])
    left = jnp.concatenate([chi, chi, clo], axis=1)
    wide = 512
    for c in range(NODES_DEV // wide):
        lanes = slice(c * wide, (c + 1) * wide)
        x = x_ref[:, lanes]
        xhi, xlo = split(x)
        zx_ref[0:K, lanes] = xhi
        zx_ref[K:2 * K, lanes] = xlo
        phi, plo = split(prev_ref[:, lanes])
        coupled = jnp.dot(left, jnp.concatenate([phi, plo, phi], axis=0), preferred_element_type=F32)
        w = x * weight_ref[:, lanes] - coupled
        for t in range(wide // TILE):
            w_ref[c * (wide // TILE) + t] = w[:, t * TILE:(t + 1) * TILE]
    zx = zx_ref[...]
    gg = lax.dot_general(zx[:K], zx, NT, preferred_element_type=F32)
    cross = gg[:, K:]
    g_ref[...] = gg[:, :K] + cross + cross.T
    table.wait()
    for copy in large:
        copy.wait()


def part_kernel(part, list_ref, count_ref, tiles_ref, *refs):
    *blocks, w_in_ref, w_ref, picked_ref = refs
    place_tiles(picked_ref, *blocks)
    multiply_part(part, list_ref, count_ref, tiles_ref, picked_ref, w_ref)


def last_kernel(list_ref, count_ref, tiles_ref, block_ref, w_in_ref, zx_ref, g_ref, w_ref, zw_ref, sums_ref, picked_ref):
    place_tiles(picked_ref, block_ref)
    multiply_part(3, list_ref, count_ref, tiles_ref, picked_ref, w_ref)
    for t in range(ROWS):
        whi, wlo = split(w_ref[t])
        zw_ref[0:K, t * TILE:(t + 1) * TILE] = whi
        zw_ref[K:2 * K, t * TILE:(t + 1) * TILE] = wlo
    zw = zw_ref[...]
    m = lax.dot_general(zx_ref[...], zw, NT, preferred_element_type=F32)
    s = lax.dot_general(zw[:K], zw, NT, preferred_element_type=F32)
    cross = s[:, K:]
    sums_ref[0:K, 0:K] = m[:K, :K] + m[:K, K:] + m[K:, :K]
    row = lax.broadcasted_iota(jnp.int32, (K, K), 0)
    col = lax.broadcasted_iota(jnp.int32, (K, K), 1)
    g = g_ref[...]
    sums_ref[0:K, K:] = jnp.where(col >= row, s[:, :K] + cross + cross.T, g)
    sums_ref[K:, 0:K] = jnp.broadcast_to(jnp.sum(jnp.where(col == row, g, 0.0), axis=0, keepdims=True), (8, K))
    sums_ref[K:, K:] = jnp.zeros((8, K), F32)


def eliminate(blocks):
    shape = blocks[0].shape
    count = len(blocks)
    sub = lax.broadcasted_iota(jnp.int32, shape, 0)
    wide = lambda v: jnp.broadcast_to(v, shape)
    done, pivots = [None] * count, []
    for start in range(0, 8 * count, 4):
        b, o = divmod(start, 8)
        head = blocks[b]
        line = [wide(head[o + j:o + j + 1, :]) for j in range(4)]
        column = [[wide(blocks[i][:, start + j:start + j + 1]) for j in range(4)] for i in range(b, count)]
        a = [[wide(column[0][l][o + j:o + j + 1, :]) for l in range(4)] for j in range(4)]
        inverse, m = [None] * 4, {}
        for j in range(4):
            inverse[j] = 1.0 / a[j][j]
            for t in range(j + 1, 4):
                m[t, j] = a[j][t] * inverse[j]
                for l in range(t, 4):
                    a[t][l] = a[t][l] - m[t, j] * a[j][l]
            for t in range(j + 1, 4):
                line[t] = line[t] - m[t, j] * line[j]
        scaled = [line[j] * inverse[j] for j in range(4)]
        for i in range(b, count):
            if i == b and o == 4:
                continue
            c = column[i - b]
            for j in range(4):
                for t in range(j + 1, 4):
                    c[t] = c[t] - m[t, j] * c[j]
            blocks[i] = blocks[i] - ((c[0] * scaled[0] + c[1] * scaled[1]) + (c[2] * scaled[2] + c[3] * scaled[3]))
        rows = blocks[b] if done[b] is None else done[b]
        for j in range(4):
            rows = jnp.where(sub == o + j, line[j] * lax.rsqrt(a[j][j]), rows)
            pivots.append(a[j][j])
        done[b] = rows
    return done, pivots


def factor_kernel(node_total, sums_ref, rayleigh_ref, r_ref, f_ref, flag_ref):
    inv = 1.0 / node_total
    r = sums_ref[0:K, 0:K] * inv
    both = sums_ref[0:K, K:] * inv
    diagonal = sums_ref[K:K + 1, 0:K] * inv
    row = lax.broadcasted_iota(jnp.int32, (K, K), 0)
    col = lax.broadcasted_iota(jnp.int32, (K, K), 1)
    eye = jnp.where(row == col, 1.0, 0.0)
    rt = r.T
    flip = both.T
    s = jnp.where(col >= row, both, flip)
    g = jnp.where(col < row, both, jnp.where(col > row, flip, diagonal))
    gram = s - dot3(rt, dot3(2.0 * eye - g, r))
    work = jnp.concatenate([gram, eye], axis=1)
    done, pivots = eliminate([work[8 * b:8 * b + 8] for b in range(K // 8)])
    work = jnp.concatenate(done, axis=0)
    lower_inv = jnp.where(col <= row, work[:, K:], 0.0)
    rayleigh_ref[...] = r
    r_ref[...] = jnp.where(col >= row, work[:, :K], 0.0)
    f_ref[:, 0:K] = lower_inv
    f_ref[:, K:] = -dot3(lower_inv, rt)
    largest = jnp.max(jnp.where(row == col, s, 0.0))
    smallest = jnp.min(functools.reduce(jnp.minimum, pivots))
    flag_ref[0] = jnp.where(smallest * WORST >= largest, 0, 1).astype(jnp.int32)


def final_kernel(f_ref, zw_ref, zx_ref, r_ref, out_hbm, r_hbm, out_ref, sems):
    copies = [pltpu.make_async_copy(r_ref, r_hbm, sems.at[CHUNKS])]
    copies[0].start()
    f1h, f1l = split(f_ref[:, 0:K])
    f2h, f2l = split(f_ref[:, K:])
    zero = jnp.zeros((K, K), BF16)
    left = jnp.concatenate([jnp.concatenate([f1h, f1h, f2h, f2h], axis=1),
                            jnp.concatenate([f1l, zero, f2l, zero], axis=1)], axis=0)
    wide = NODES_DEV // CHUNKS
    for c in range(CHUNKS):
        lanes = slice(c * wide, (c + 1) * wide)
        z = jnp.concatenate([zw_ref[:, lanes], zx_ref[:, lanes]], axis=0)
        y = jnp.dot(left, z, preferred_element_type=F32)
        out_ref[:, lanes] = y[:K] + y[K:]
        copies.append(pltpu.make_async_copy(out_ref.at[:, lanes], out_hbm.at[:, lanes], sems.at[c]))
        copies[-1].start()
    for copy in copies:
        copy.wait()


def exchange(v, axis, to):
    n = lax.axis_size(axis)
    return lax.ppermute(v, axis, [(i, to(i)) for i in range(n)])


def core_swap(v):
    return exchange(v, "row", lambda i: i ^ 1)


def onward(v, way):
    return exchange(v, "row", lambda i: (i + (2 * way if i % 2 == 0 else -2 * way)) % 8)


def total(v):
    v = v + core_swap(v)
    for axis, unit in (("row", 2), ("col", 1), ("col", 4)):
        others = [exchange(v, axis, lambda i, d=d * unit: i ^ d) for d in (1, 2, 3)]
        v = (v + others[0]) + (others[1] + others[2])
    return v


def local(tile_blocks, tile_column, row_degree, node_weight, block_now, block_prev, coupling):
    node_total = NODES_DEV * lax.axis_size("row") * lax.axis_size("col")
    after = lax.optimization_barrier
    slab_vmem = pltpu.VMEM(SLAB, F32)
    pair_vmem = pltpu.VMEM((2 * K, NODES_DEV), BF16)
    square = jax.ShapeDtypeStruct((K, K), F32)

    half, x = call(
        round_kernel, "round_block", (pltpu.VMEM(SLAB, BF16), pltpu.VMEM((K, NODES_DEV), F32)), [hbm()],
        (vmem(), vmem()), 8, 1, [pltpu.SemaphoreType.DMA((4,))])(in_hbm(block_now.T))
    a1 = onward(half, 1)
    a2 = onward(half, -1)
    sib = core_swap(half)
    tiles, w, zx, g, lists, counts = call(
        prepare_kernel, "prepare",
        (pltpu.VMEM((SLOTS, TILE, TILE), BF16), slab_vmem, pair_vmem, pltpu.VMEM((K, K), F32),
         pltpu.SMEM((1, PARTS * LIST), jnp.int32), pltpu.SMEM((PARTS,), jnp.int32)),
        [hbm()] * 6 + [vmem()], (vmem(), vmem(), vmem(), vmem(), smem(), smem()), 16, 7,
        [pltpu.VMEM((1, SLOTS), jnp.int32), pltpu.VMEM((1, ROWS), jnp.int32), pltpu.VMEM((K, NODES_DEV), F32),
         pltpu.VMEM((1, NODES_DEV), F32), pltpu.VMEM((K, K), F32), pltpu.VMEM((1, PARTS * LIST), jnp.int32),
         pltpu.SemaphoreType.DMA((6,)), pltpu.SemaphoreType.DMA((CHUNKS,))])(
            in_hbm(tile_blocks), in_hbm(tile_column.reshape(1, SLOTS)), in_hbm(row_degree.reshape(1, ROWS)),
            in_hbm(block_prev.T), in_hbm(node_weight.reshape(1, NODES_DEV)), in_hbm(coupling), x)

    def add_part(part, name, blocks, w, us):
        n = len(blocks)
        count = sum(block.shape[0] for block in blocks)
        return call(functools.partial(part_kernel, part), name, slab_vmem, [smem(), smem()] + [vmem()] * (n + 2),
                    vmem(), 12, us, [pltpu.VMEM((1 + count, K, TILE), BF16)], {3 + n: 0})(
                        lists, counts, tiles, *blocks, w)

    a1, a2, w = after((a1, a2, w))
    a3 = onward(a1, 1)
    h = ROWS // 2
    b1 = [core_swap(a1[:h]), core_swap(a1[h:])]
    b2 = [core_swap(a2[:h]), core_swap(a2[h:])]
    w = add_part(0, "near_parts", [half, sib, a1] + b1, w, 5)
    w = add_part(1, "late_part", [a2] + b2, w, 3)
    a3, w = after((a3, w))
    b3 = core_swap(a3)
    w = add_part(2, "far_part", [a3], w, 2)
    _, zw, sums = call(
        last_kernel, "last_part", (slab_vmem, pair_vmem, jax.ShapeDtypeStruct((K + 8, 2 * K), F32)),
        [smem(), smem()] + [vmem()] * 5, (vmem(), vmem(), vmem()), 16, 4,
        [pltpu.VMEM((1 + ROWS, K, TILE), BF16)], {4: 0})(lists, counts, tiles, b3, w, zx, g)

    sums = total(sums)
    rayleigh, r_factor, f, flag = call(
        functools.partial(factor_kernel, node_total), "factor",
        (square, square, jax.ShapeDtypeStruct((K, 2 * K), F32), jax.ShapeDtypeStruct((1,), jnp.int32)),
        [vmem()], (vmem(), vmem(), vmem(), smem()), 8, 5)(sums)

    def plain(zw, zx, f, sums, r_factor):
        return call(
            final_kernel, "scale_block", (pltpu.HBM((K, NODES_DEV), F32), pltpu.HBM((K, K), F32)), [vmem()] * 4,
            (hbm(), hbm()), 12, 2, [pltpu.VMEM((K, NODES_DEV), F32), pltpu.SemaphoreType.DMA((CHUNKS + 1,))])(
                f, zw, zx, r_factor)

    def two_passes(zw, zx, f, sums, r_factor):
        whole = lambda z: z[:K].astype(F32) + z[K:].astype(F32)
        rayleigh_t = sums[:K, :K].T / node_total
        w_next = whole(zw) - jnp.dot(rayleigh_t, whole(zx), precision=HIGHEST)
        gram = total(jnp.dot(w_next, w_next.T, precision=HIGHEST)) / node_total
        lower = jnp.linalg.cholesky(gram)
        return jax.scipy.linalg.solve_triangular(lower, w_next, lower=True), lower.T

    out, r_factor = lax.cond(flag[0] == 0, plain, two_passes, zw, zx, f, sums, r_factor)
    return out.T, rayleigh, r_factor


def solution(mesh):
    in_specs = (
        P(("row", "col"), None, None),
        P(("row", "col")),
        P(("row", "col")),
        P(("row", "col")),
        P(("row", "col"), None),
        P(("row", "col"), None),
        P(),
    )
    out_specs = (P(("row", "col"), None), P(), P())
    return jax.shard_map(local, mesh=mesh, in_specs=in_specs, out_specs=out_specs, check_vma=False)
```

```python
import functools
import jax
import jax.numpy as jnp
from jax import lax
from jax.experimental import pallas as pl
from jax.experimental.pallas import tpu as pltpu
from jax.sharding import PartitionSpec as P

TILE = 128
K = 64
ROWS = 32
SLOTS = 512
NODES_DEV = ROWS * TILE
UNROLL = 8
LIST = 614
PARTS = 5
TABLE = 3072
CHUNKS = 8
WORST = 32.0
F32 = jnp.float32
BF16 = jnp.bfloat16
NT = (((1,), (1,)), ((), ()))
HIGHEST = lax.Precision.HIGHEST
SLAB = (ROWS, K, TILE)


def vmem():
    return pl.BlockSpec(memory_space=pltpu.VMEM)


def smem():
    return pl.BlockSpec(memory_space=pltpu.SMEM)


def hbm():
    return pl.BlockSpec(memory_space=pltpu.HBM)


def in_hbm(x):
    return pltpu.with_memory_space_constraint(x, pltpu.HBM)


def call(kernel, name, out_shape, in_specs, out_specs, mib, us, scratch=(), aliases=None):
    return pl.pallas_call(
        kernel, out_shape=out_shape, in_specs=in_specs, out_specs=out_specs, scratch_shapes=list(scratch), name=name,
        input_output_aliases=aliases or {},
        compiler_params=pltpu.CompilerParams(vmem_limit_bytes=mib << 20),
        cost_estimate=pl.CostEstimate(flops=int(us * 1e9), bytes_accessed=int(us * 3e6), transcendentals=0))


def split(x):
    hi = x.astype(BF16)
    return hi, (x - hi.astype(F32)).astype(BF16)


def dot3(a, b):
    ah, al = split(a)
    bh, bl = split(b)
    return jnp.dot(jnp.concatenate([ah, ah, al], axis=1), jnp.concatenate([bh, bl, bh], axis=0),
                   preferred_element_type=F32)


def round_kernel(x_hbm, half_ref, x_ref, sems):
    wide = NODES_DEV // 4
    copies = [pltpu.make_async_copy(x_hbm.at[:, c * wide:(c + 1) * wide], x_ref.at[:, c * wide:(c + 1) * wide],
                                    sems.at[c]) for c in range(4)]
    for copy in copies:
        copy.start()
    for c, copy in enumerate(copies):
        copy.wait()
        for t in range(c * wide // TILE, (c + 1) * wide // TILE):
            half_ref[t] = x_ref[:, t * TILE:(t + 1) * TILE].astype(BF16)


def build_lists(column, degree, table_ref, count_ref):
    member_row = lax.axis_index("row")
    z = lax.shift_right_logical(member_row, 1)
    core = member_row & 1
    from_z = (z + 3 + 2 * core) & 3
    peer = lax.shift_right_logical(column, 9)
    peer_z = lax.shift_right_logical(peer, 1)
    dz = (peer_z - z) & 3
    dc = (peer & 1) ^ core
    side = jnp.where(peer_z == from_z, 1, 0)
    odd = (dz & 1) == 1
    part = jnp.where(odd, 1 + dc, jnp.where(dz == 0, 0, 3 + dc))
    offset = jnp.where(odd, jnp.where(side == dc, 32, 0), jnp.where(dz == 0, 32 * dc, 0))
    tile = 1 + (column & 31) + offset
    r_i = lax.broadcasted_iota(jnp.int32, (ROWS, ROWS), 0)
    r_j = lax.broadcasted_iota(jnp.int32, (ROWS, ROWS), 1)
    degrees = jnp.broadcast_to(degree, (ROWS, ROWS))
    starts = jnp.sum(jnp.where(r_j < r_i, degrees, 0), axis=1, keepdims=True)
    ends = jnp.sum(jnp.where(r_j <= r_i, degrees, 0), axis=1, keepdims=True)
    s = lax.broadcasted_iota(jnp.int32, (ROWS, SLOTS), 1)
    member = jnp.where((s >= starts) & (s < ends), 1.0, 0.0)
    row = jnp.sum(member * lax.broadcasted_iota(jnp.int32, (ROWS, SLOTS), 0).astype(F32), axis=0, keepdims=True)
    used = jnp.sum(member, axis=0, keepdims=True)
    member = member.astype(BF16)
    line = lax.broadcasted_iota(jnp.int32, (8, SLOTS), 0)
    mine = jnp.where((line == part) & (used > 0.5), 1.0, 0.0)
    mine_half = mine.astype(BF16)
    s_i = lax.broadcasted_iota(jnp.int32, (SLOTS, SLOTS), 0)
    s_j = lax.broadcasted_iota(jnp.int32, (SLOTS, SLOTS), 1)
    before = jnp.where(s_i < s_j, 1.0, 0.0).astype(BF16)
    rank = jnp.dot(mine_half, before, preferred_element_type=F32)
    per_row = lax.dot_general(mine_half, member, NT, preferred_element_type=F32).astype(jnp.int32)
    pad = per_row & 1
    earlier = jnp.where(r_i < r_j, 1.0, 0.0).astype(BF16)
    pads = jnp.dot(pad.astype(F32).astype(BF16), earlier, preferred_element_type=F32)
    shift = jnp.dot(pads.astype(BF16), member, preferred_element_type=F32)
    base = (line * LIST).astype(F32)
    place = (jnp.sum(mine * (rank + shift + base + 1.0), axis=0, keepdims=True) - 1.0).astype(jnp.int32)
    slot = lax.broadcasted_iota(jnp.int32, (1, SLOTS), 1)
    values = jnp.where(line == 0, tile, jnp.where(line == 1, slot & 31, jnp.where(
        line == 2, lax.shift_right_logical(slot, 5), row.astype(jnp.int32))))
    values = values.astype(F32).astype(BF16)
    for c in range(TABLE // 256):
        at = lax.broadcasted_iota(jnp.int32, (256, SLOTS), 0) + c * 256
        hot = jnp.where(at == place, 1.0, 0.0).astype(BF16)
        got = lax.dot_general(values, hot, NT, preferred_element_type=F32).astype(jnp.int32)
        table_ref[0:1, c * 256:(c + 1) * 256] = got[0:1] | (got[1:2] << 10) | (got[2:3] << 15) | (got[3:4] << 20)
    length = jnp.sum(per_row + pad, axis=1, keepdims=True)
    first = lax.broadcasted_iota(jnp.int32, (8, 1), 0)
    for p in range(PARTS):
        n = jnp.sum(jnp.where(first == p, length, 0))
        count_ref[p] = lax.div(n + 2 * UNROLL - 1, 2 * UNROLL)


def multiply_part(part, list_ref, count_ref, tiles_ref, picked_ref, w_ref):
    def group(g, carry):
        base = part * LIST + g * (2 * UNROLL)
        rows, products = [], []
        for u in range(UNROLL):
            first, second = list_ref[0, base + 2 * u], list_ref[0, base + 2 * u + 1]
            x = [picked_ref[e & 255] for e in (first, second)]
            a = [tiles_ref[lax.shift_right_logical(e, 10) & 511] for e in (first, second)]
            rows.append(lax.shift_right_logical(first, 20))
            products.append(lax.dot_general(
                jnp.concatenate(x, axis=1), jnp.concatenate(a, axis=1), NT, preferred_element_type=F32))
        for row, product in zip(rows, products):
            w_ref[row] += product
        return carry

    lax.fori_loop(0, count_ref[part], group, 0)


def place_tiles(picked_ref, *blocks):
    picked_ref[0] = jnp.zeros((K, TILE), BF16)
    at = 1
    for block in blocks:
        picked_ref[at:at + block.shape[0]] = block[...]
        at += block.shape[0]


def tile_copies(tiles_hbm, tiles_ref, sems):
    n = SLOTS // CHUNKS
    spans = [slice(c * n, (c + 1) * n) for c in range(CHUNKS)]
    return [pltpu.make_async_copy(tiles_hbm.at[span], tiles_ref.at[span], sems.at[c]) for c, span in enumerate(spans)]


def prepare_kernel(tiles_hbm, column_hbm, degree_hbm, prev_hbm, weight_hbm, coupling_hbm, x_ref,
                   half_ref, sib_ref, tiles_ref, w_ref, zx_ref, g_ref, list_ref, count_ref,
                   column_ref, degree_ref, prev_ref, weight_ref, coupling_ref, table_ref, picked_ref, sems,
                   tile_sems):
    small = [pltpu.make_async_copy(a, b, sems.at[i]) for i, (a, b) in enumerate((
        (column_hbm, column_ref), (degree_hbm, degree_ref), (coupling_hbm, coupling_ref), (weight_hbm, weight_ref),
        (prev_hbm, prev_ref)))]
    large = tile_copies(tiles_hbm, tiles_ref, tile_sems)
    for copy in small + large:
        copy.start()
    small[0].wait()
    small[1].wait()
    build_lists(column_ref[...], degree_ref[...], table_ref, count_ref)
    table = pltpu.make_async_copy(table_ref, list_ref, sems.at[5])
    table.start()
    for copy in small[2:]:
        copy.wait()
    chi, clo = split(coupling_ref[...])
    left = jnp.concatenate([chi, chi, clo], axis=1)
    wide = 512
    for c in range(NODES_DEV // wide):
        lanes = slice(c * wide, (c + 1) * wide)
        x = x_ref[:, lanes]
        xhi, xlo = split(x)
        zx_ref[0:K, lanes] = xhi
        zx_ref[K:2 * K, lanes] = xlo
        phi, plo = split(prev_ref[:, lanes])
        coupled = jnp.dot(left, jnp.concatenate([phi, plo, phi], axis=0), preferred_element_type=F32)
        w = x * weight_ref[:, lanes] - coupled
        for t in range(wide // TILE):
            w_ref[c * (wide // TILE) + t] = w[:, t * TILE:(t + 1) * TILE]
    zx = zx_ref[...]
    gg = lax.dot_general(zx[:K], zx, NT, preferred_element_type=F32)
    cross = gg[:, K:]
    g_ref[...] = gg[:, :K] + cross + cross.T
    place_tiles(picked_ref, half_ref, sib_ref)
    table.wait()
    for copy in large:
        copy.wait()
    multiply_part(0, list_ref, count_ref, tiles_ref, picked_ref, w_ref)


def part_kernel(part, list_ref, count_ref, tiles_ref, *refs):
    *blocks, w_in_ref, w_ref, picked_ref = refs
    place_tiles(picked_ref, *blocks)
    multiply_part(part, list_ref, count_ref, tiles_ref, picked_ref, w_ref)


def last_kernel(list_ref, count_ref, tiles_ref, block_ref, w_in_ref, zx_ref, g_ref, w_ref, zw_ref, sums_ref, picked_ref):
    place_tiles(picked_ref, block_ref)
    multiply_part(4, list_ref, count_ref, tiles_ref, picked_ref, w_ref)
    for t in range(ROWS):
        whi, wlo = split(w_ref[t])
        zw_ref[0:K, t * TILE:(t + 1) * TILE] = whi
        zw_ref[K:2 * K, t * TILE:(t + 1) * TILE] = wlo
    zw = zw_ref[...]
    m = lax.dot_general(zx_ref[...], zw, NT, preferred_element_type=F32)
    s = lax.dot_general(zw[:K], zw, NT, preferred_element_type=F32)
    cross = s[:, K:]
    sums_ref[0:K, 0:K] = m[:K, :K] + m[:K, K:] + m[K:, :K]
    row = lax.broadcasted_iota(jnp.int32, (K, K), 0)
    col = lax.broadcasted_iota(jnp.int32, (K, K), 1)
    g = g_ref[...]
    sums_ref[0:K, K:] = jnp.where(col >= row, s[:, :K] + cross + cross.T, g)
    sums_ref[K:, 0:K] = jnp.broadcast_to(jnp.sum(jnp.where(col == row, g, 0.0), axis=0, keepdims=True), (8, K))
    sums_ref[K:, K:] = jnp.zeros((8, K), F32)


def eliminate(blocks):
    shape = blocks[0].shape
    count = len(blocks)
    sub = lax.broadcasted_iota(jnp.int32, shape, 0)
    wide = lambda v: jnp.broadcast_to(v, shape)
    done, pivots = [None] * count, []
    for start in range(0, 8 * count, 4):
        b, o = divmod(start, 8)
        head = blocks[b]
        line = [wide(head[o + j:o + j + 1, :]) for j in range(4)]
        column = [[wide(blocks[i][:, start + j:start + j + 1]) for j in range(4)] for i in range(b, count)]
        a = [[wide(column[0][l][o + j:o + j + 1, :]) for l in range(4)] for j in range(4)]
        inverse, m = [None] * 4, {}
        for j in range(4):
            inverse[j] = 1.0 / a[j][j]
            for t in range(j + 1, 4):
                m[t, j] = a[j][t] * inverse[j]
                for l in range(t, 4):
                    a[t][l] = a[t][l] - m[t, j] * a[j][l]
            for t in range(j + 1, 4):
                line[t] = line[t] - m[t, j] * line[j]
        scaled = [line[j] * inverse[j] for j in range(4)]
        for i in range(b, count):
            if i == b and o == 4:
                continue
            c = column[i - b]
            for j in range(4):
                for t in range(j + 1, 4):
                    c[t] = c[t] - m[t, j] * c[j]
            blocks[i] = blocks[i] - ((c[0] * scaled[0] + c[1] * scaled[1]) + (c[2] * scaled[2] + c[3] * scaled[3]))
        rows = blocks[b] if done[b] is None else done[b]
        for j in range(4):
            rows = jnp.where(sub == o + j, line[j] * lax.rsqrt(a[j][j]), rows)
            pivots.append(a[j][j])
        done[b] = rows
    return done, pivots


def factor_kernel(node_total, sums_ref, rayleigh_ref, r_ref, f_ref, flag_ref):
    inv = 1.0 / node_total
    r = sums_ref[0:K, 0:K] * inv
    both = sums_ref[0:K, K:] * inv
    diagonal = sums_ref[K:K + 1, 0:K] * inv
    row = lax.broadcasted_iota(jnp.int32, (K, K), 0)
    col = lax.broadcasted_iota(jnp.int32, (K, K), 1)
    eye = jnp.where(row == col, 1.0, 0.0)
    rt = r.T
    flip = both.T
    s = jnp.where(col >= row, both, flip)
    g = jnp.where(col < row, both, jnp.where(col > row, flip, diagonal))
    gram = s - dot3(rt, dot3(2.0 * eye - g, r))
    work = jnp.concatenate([gram, eye], axis=1)
    done, pivots = eliminate([work[8 * b:8 * b + 8] for b in range(K // 8)])
    work = jnp.concatenate(done, axis=0)
    lower_inv = jnp.where(col <= row, work[:, K:], 0.0)
    rayleigh_ref[...] = r
    r_ref[...] = jnp.where(col >= row, work[:, :K], 0.0)
    f_ref[:, 0:K] = lower_inv
    f_ref[:, K:] = -dot3(lower_inv, rt)
    largest = jnp.max(jnp.where(row == col, s, 0.0))
    smallest = jnp.min(functools.reduce(jnp.minimum, pivots))
    flag_ref[0] = jnp.where(smallest * WORST >= largest, 0, 1).astype(jnp.int32)


def final_kernel(f_ref, zw_ref, zx_ref, r_ref, out_hbm, r_hbm, out_ref, sems):
    copies = [pltpu.make_async_copy(r_ref, r_hbm, sems.at[CHUNKS])]
    copies[0].start()
    f1h, f1l = split(f_ref[:, 0:K])
    f2h, f2l = split(f_ref[:, K:])
    zero = jnp.zeros((K, K), BF16)
    left = jnp.concatenate([jnp.concatenate([f1h, f1h, f2h, f2h], axis=1),
                            jnp.concatenate([f1l, zero, f2l, zero], axis=1)], axis=0)
    wide = NODES_DEV // CHUNKS
    for c in range(CHUNKS):
        lanes = slice(c * wide, (c + 1) * wide)
        z = jnp.concatenate([zw_ref[:, lanes], zx_ref[:, lanes]], axis=0)
        y = jnp.dot(left, z, preferred_element_type=F32)
        out_ref[:, lanes] = y[:K] + y[K:]
        copies.append(pltpu.make_async_copy(out_ref.at[:, lanes], out_hbm.at[:, lanes], sems.at[c]))
        copies[-1].start()
    for copy in copies:
        copy.wait()


def exchange(v, axis, to):
    n = lax.axis_size(axis)
    return lax.ppermute(v, axis, [(i, to(i)) for i in range(n)])


def core_swap(v):
    return exchange(v, "row", lambda i: i ^ 1)


def onward(v, way):
    return exchange(v, "row", lambda i: (i + (2 * way if i % 2 == 0 else -2 * way)) % 8)


def total(v):
    v = v + core_swap(v)
    for axis, unit in (("row", 2), ("col", 1), ("col", 4)):
        others = [exchange(v, axis, lambda i, d=d * unit: i ^ d) for d in (1, 2, 3)]
        v = (v + others[0]) + (others[1] + others[2])
    return v


def local(tile_blocks, tile_column, row_degree, node_weight, block_now, block_prev, coupling):
    node_total = NODES_DEV * lax.axis_size("row") * lax.axis_size("col")
    after = lax.optimization_barrier
    slab_vmem = pltpu.VMEM(SLAB, F32)
    pair_vmem = pltpu.VMEM((2 * K, NODES_DEV), BF16)
    square = jax.ShapeDtypeStruct((K, K), F32)

    half, x = call(
        round_kernel, "round_block", (pltpu.VMEM(SLAB, BF16), pltpu.VMEM((K, NODES_DEV), F32)), [hbm()],
        (vmem(), vmem()), 8, 1, [pltpu.SemaphoreType.DMA((4,))])(in_hbm(block_now.T))
    a1 = onward(half, 1)
    a2 = onward(half, -1)
    sib = core_swap(half)
    tiles, w, zx, g, lists, counts = call(
        prepare_kernel, "prepare",
        (pltpu.VMEM((SLOTS, TILE, TILE), BF16), slab_vmem, pair_vmem, pltpu.VMEM((K, K), F32),
         pltpu.SMEM((1, TABLE), jnp.int32), pltpu.SMEM((PARTS,), jnp.int32)),
        [hbm()] * 6 + [vmem()] * 3, (vmem(), vmem(), vmem(), vmem(), smem(), smem()), 16, 9,
        [pltpu.VMEM((1, SLOTS), jnp.int32), pltpu.VMEM((1, ROWS), jnp.int32), pltpu.VMEM((K, NODES_DEV), F32),
         pltpu.VMEM((1, NODES_DEV), F32), pltpu.VMEM((K, K), F32), pltpu.VMEM((1, TABLE), jnp.int32),
         pltpu.VMEM((1 + 2 * ROWS, K, TILE), BF16), pltpu.SemaphoreType.DMA((6,)), pltpu.SemaphoreType.DMA((CHUNKS,))])(
            in_hbm(tile_blocks), in_hbm(tile_column.reshape(1, SLOTS)), in_hbm(row_degree.reshape(1, ROWS)),
            in_hbm(block_prev.T), in_hbm(node_weight.reshape(1, NODES_DEV)), in_hbm(coupling), x, half, sib)

    def add_part(part, name, blocks, w, us):
        n = len(blocks)
        count = sum(block.shape[0] for block in blocks)
        return call(functools.partial(part_kernel, part), name, slab_vmem, [smem(), smem()] + [vmem()] * (n + 2),
                    vmem(), 12, us, [pltpu.VMEM((1 + count, K, TILE), BF16)], {3 + n: 0})(
                        lists, counts, tiles, *blocks, w)

    a1, a2, w = after((a1, a2, w))
    a3 = onward(a1, 1)
    b1 = core_swap(a1)
    b2 = core_swap(a2)
    w = add_part(1, "near_part", [a1, a2], w, 8)
    w = add_part(2, "near_swapped", [b1, b2], w, 0)
    a3, w = after((a3, w))
    b3 = core_swap(a3)
    w = add_part(3, "far_part", [a3], w, 2)
    _, zw, sums = call(
        last_kernel, "last_part", (slab_vmem, pair_vmem, jax.ShapeDtypeStruct((K + 8, 2 * K), F32)),
        [smem(), smem()] + [vmem()] * 5, (vmem(), vmem(), vmem()), 16, 4,
        [pltpu.VMEM((1 + ROWS, K, TILE), BF16)], {4: 0})(lists, counts, tiles, b3, w, zx, g)

    sums = total(sums)
    rayleigh, r_factor, f, flag = call(
        functools.partial(factor_kernel, node_total), "factor",
        (square, square, jax.ShapeDtypeStruct((K, 2 * K), F32), jax.ShapeDtypeStruct((1,), jnp.int32)),
        [vmem()], (vmem(), vmem(), vmem(), smem()), 8, 5)(sums)

    def plain(zw, zx, f, sums, r_factor):
        return call(
            final_kernel, "scale_block", (pltpu.HBM((K, NODES_DEV), F32), pltpu.HBM((K, K), F32)), [vmem()] * 4,
            (hbm(), hbm()), 12, 2, [pltpu.VMEM((K, NODES_DEV), F32), pltpu.SemaphoreType.DMA((CHUNKS + 1,))])(
                f, zw, zx, r_factor)

    def two_passes(zw, zx, f, sums, r_factor):
        whole = lambda z: z[:K].astype(F32) + z[K:].astype(F32)
        rayleigh_t = sums[:K, :K].T / node_total
        w_next = whole(zw) - jnp.dot(rayleigh_t, whole(zx), precision=HIGHEST)
        gram = total(jnp.dot(w_next, w_next.T, precision=HIGHEST)) / node_total
        lower = jnp.linalg.cholesky(gram)
        return jax.scipy.linalg.solve_triangular(lower, w_next, lower=True), lower.T

    out, r_factor = lax.cond(flag[0] == 0, plain, two_passes, zw, zx, f, sums, r_factor)
    return out.T, rayleigh, r_factor


def solution(mesh):
    in_specs = (
        P(("row", "col"), None, None),
        P(("row", "col")),
        P(("row", "col")),
        P(("row", "col")),
        P(("row", "col"), None),
        P(("row", "col"), None),
        P(),
    )
    out_specs = (P(("row", "col"), None), P(), P())
    return jax.shard_map(local, mesh=mesh, in_specs=in_specs, out_specs=out_specs, check_vma=False)
```

```python
import functools
import jax
import jax.numpy as jnp
from jax import lax
from jax.experimental import pallas as pl
from jax.experimental.pallas import tpu as pltpu
from jax.sharding import PartitionSpec as P

TILE = 128
K = 64
ROWS = 32
SLOTS = 512
NODES_DEV = ROWS * TILE
UNROLL = 16
LIST = 614
PARTS = 5
TABLE = 3072
CHUNKS = 8
WORST = 32.0
F32 = jnp.float32
BF16 = jnp.bfloat16
NT = (((1,), (1,)), ((), ()))
HIGHEST = lax.Precision.HIGHEST
SLAB = (ROWS, K, TILE)
NODE_ROWS = (ROWS, TILE, K)


def vmem():
    return pl.BlockSpec(memory_space=pltpu.VMEM)


def smem():
    return pl.BlockSpec(memory_space=pltpu.SMEM)


def hbm():
    return pl.BlockSpec(memory_space=pltpu.HBM)


def in_hbm(x):
    return pltpu.with_memory_space_constraint(x, pltpu.HBM)


def call(kernel, name, out_shape, in_specs, out_specs, mib, us, scratch=(), aliases=None):
    return pl.pallas_call(
        kernel, out_shape=out_shape, in_specs=in_specs, out_specs=out_specs, scratch_shapes=list(scratch), name=name,
        input_output_aliases=aliases or {},
        compiler_params=pltpu.CompilerParams(vmem_limit_bytes=mib << 20),
        cost_estimate=pl.CostEstimate(flops=int(us * 1e9), bytes_accessed=int(us * 3e6), transcendentals=0))


def split(x):
    hi = x.astype(BF16)
    return hi, (x - hi.astype(F32)).astype(BF16)


def dot3(a, b):
    ah, al = split(a)
    bh, bl = split(b)
    return jnp.dot(jnp.concatenate([ah, ah, al], axis=1), jnp.concatenate([bh, bl, bh], axis=0),
                   preferred_element_type=F32)


def round_kernel(x_hbm, half_ref, x_ref, sems):
    wide = NODES_DEV // 4
    copies = [pltpu.make_async_copy(x_hbm.at[:, c * wide:(c + 1) * wide], x_ref.at[:, c * wide:(c + 1) * wide],
                                    sems.at[c]) for c in range(4)]
    for copy in copies:
        copy.start()
    for c, copy in enumerate(copies):
        copy.wait()
        for t in range(c * wide // TILE, (c + 1) * wide // TILE):
            half_ref[t] = x_ref[:, t * TILE:(t + 1) * TILE].astype(BF16)


def build_lists(column, degree, table_ref, count_ref):
    member_row = lax.axis_index("row")
    z = lax.shift_right_logical(member_row, 1)
    core = member_row & 1
    from_z = (z + 3 + 2 * core) & 3
    peer = lax.shift_right_logical(column, 9)
    peer_z = lax.shift_right_logical(peer, 1)
    dz = (peer_z - z) & 3
    dc = (peer & 1) ^ core
    side = jnp.where(peer_z == from_z, 1, 0)
    odd = (dz & 1) == 1
    part = jnp.where(odd, 1 + dc, jnp.where(dz == 0, dc, 3 + dc))
    offset = jnp.where(odd, jnp.where(side == dc, 32, 0), jnp.where(dz == 0, 64 * dc, 0))
    tile = 1 + (column & 31) + offset
    r_i = lax.broadcasted_iota(jnp.int32, (ROWS, ROWS), 0)
    r_j = lax.broadcasted_iota(jnp.int32, (ROWS, ROWS), 1)
    degrees = jnp.broadcast_to(degree, (ROWS, ROWS))
    starts = jnp.sum(jnp.where(r_j < r_i, degrees, 0), axis=1, keepdims=True)
    ends = jnp.sum(jnp.where(r_j <= r_i, degrees, 0), axis=1, keepdims=True)
    s = lax.broadcasted_iota(jnp.int32, (ROWS, SLOTS), 1)
    member = jnp.where((s >= starts) & (s < ends), 1.0, 0.0)
    row = jnp.sum(member * lax.broadcasted_iota(jnp.int32, (ROWS, SLOTS), 0).astype(F32), axis=0, keepdims=True)
    used = jnp.sum(member, axis=0, keepdims=True)
    member = member.astype(BF16)
    line = lax.broadcasted_iota(jnp.int32, (8, SLOTS), 0)
    mine = jnp.where((line == part) & (used > 0.5), 1.0, 0.0)
    mine_half = mine.astype(BF16)
    s_i = lax.broadcasted_iota(jnp.int32, (SLOTS, SLOTS), 0)
    s_j = lax.broadcasted_iota(jnp.int32, (SLOTS, SLOTS), 1)
    before = jnp.where(s_i < s_j, 1.0, 0.0).astype(BF16)
    rank = jnp.dot(mine_half, before, preferred_element_type=F32)
    per_row = lax.dot_general(mine_half, member, NT, preferred_element_type=F32).astype(jnp.int32)
    pad = per_row & 1
    earlier = jnp.where(r_i < r_j, 1.0, 0.0).astype(BF16)
    pads = jnp.dot(pad.astype(F32).astype(BF16), earlier, preferred_element_type=F32)
    shift = jnp.dot(pads.astype(BF16), member, preferred_element_type=F32)
    base = (line * LIST).astype(F32)
    place = (jnp.sum(mine * (rank + shift + base + 1.0), axis=0, keepdims=True) - 1.0).astype(jnp.int32)
    slot = lax.broadcasted_iota(jnp.int32, (1, SLOTS), 1)
    values = jnp.where(line == 0, tile, jnp.where(line == 1, slot & 31, jnp.where(
        line == 2, lax.shift_right_logical(slot, 5), row.astype(jnp.int32))))
    values = values.astype(F32).astype(BF16)
    for c in range(TABLE // 256):
        at = lax.broadcasted_iota(jnp.int32, (256, SLOTS), 0) + c * 256
        hot = jnp.where(at == place, 1.0, 0.0).astype(BF16)
        got = lax.dot_general(values, hot, NT, preferred_element_type=F32).astype(jnp.int32)
        table_ref[0:1, c * 256:(c + 1) * 256] = got[0:1] | (got[1:2] << 10) | (got[2:3] << 15) | (got[3:4] << 20)
    length = jnp.sum(per_row + pad, axis=1, keepdims=True)
    first = lax.broadcasted_iota(jnp.int32, (8, 1), 0)
    for p in range(PARTS):
        n = jnp.sum(jnp.where(first == p, length, 0))
        count_ref[p] = lax.div(n + 2 * UNROLL - 1, 2 * UNROLL)


def multiply_part(part, list_ref, count_ref, tiles_ref, picked_ref, w_ref):
    def group(g, carry):
        base = part * LIST + g * (2 * UNROLL)
        rows, products = [], []
        for u in range(UNROLL):
            first, second = list_ref[0, base + 2 * u], list_ref[0, base + 2 * u + 1]
            x = [picked_ref[e & 255] for e in (first, second)]
            a = [tiles_ref[lax.shift_right_logical(e, 10) & 511] for e in (first, second)]
            rows.append(lax.shift_right_logical(first, 20))
            products.append(lax.dot_general(
                jnp.concatenate(a, axis=1), jnp.concatenate(x, axis=1), NT, preferred_element_type=F32))
        for row, product in zip(rows, products):
            w_ref[row] += product
        return carry

    lax.fori_loop(0, count_ref[part], group, 0)


def place_tiles(picked_ref, *blocks):
    picked_ref[0] = jnp.zeros((K, TILE), BF16)
    at = 1
    for block in blocks:
        picked_ref[at:at + block.shape[0]] = block[...]
        at += block.shape[0]


def tile_copies(tiles_hbm, tiles_ref, sems):
    n = SLOTS // CHUNKS
    spans = [slice(c * n, (c + 1) * n) for c in range(CHUNKS)]
    return [pltpu.make_async_copy(tiles_hbm.at[span], tiles_ref.at[span], sems.at[c]) for c, span in enumerate(spans)]


def prepare_kernel(tiles_hbm, column_hbm, degree_hbm, prev_hbm, weight_hbm, coupling_hbm, x_ref,
                   half_ref, tiles_ref, w_ref, zx_ref, g_ref, list_ref, count_ref,
                   column_ref, degree_ref, prev_ref, weight_ref, coupling_ref, table_ref, picked_ref, sems,
                   tile_sems):
    small = [pltpu.make_async_copy(a, b, sems.at[i]) for i, (a, b) in enumerate((
        (column_hbm, column_ref), (degree_hbm, degree_ref), (coupling_hbm, coupling_ref), (weight_hbm, weight_ref),
        (prev_hbm, prev_ref)))]
    large = tile_copies(tiles_hbm, tiles_ref, tile_sems)
    for copy in small + large:
        copy.start()
    small[0].wait()
    small[1].wait()
    build_lists(column_ref[...], degree_ref[...], table_ref, count_ref)
    table = pltpu.make_async_copy(table_ref, list_ref, sems.at[5])
    table.start()
    for copy in small[2:]:
        copy.wait()
    chi, clo = split(coupling_ref[...])
    left = jnp.concatenate([chi, chi, clo], axis=1)
    wide = 512
    for c in range(NODES_DEV // wide):
        lanes = slice(c * wide, (c + 1) * wide)
        x = x_ref[:, lanes]
        xhi, xlo = split(x)
        zx_ref[0:K, lanes] = xhi
        zx_ref[K:2 * K, lanes] = xlo
        phi, plo = split(prev_ref[:, lanes])
        coupled = jnp.dot(left, jnp.concatenate([phi, plo, phi], axis=0), preferred_element_type=F32)
        w = x * weight_ref[:, lanes] - coupled
        for t in range(wide // TILE):
            w_ref[c * (wide // TILE) + t] = w[:, t * TILE:(t + 1) * TILE].T
    zx = zx_ref[...]
    gg = lax.dot_general(zx[:K], zx, NT, preferred_element_type=F32)
    cross = gg[:, K:]
    g_ref[...] = gg[:, :K] + cross + cross.T
    place_tiles(picked_ref, half_ref)
    table.wait()
    for copy in large:
        copy.wait()
    multiply_part(0, list_ref, count_ref, tiles_ref, picked_ref, w_ref)


def part_kernel(part, list_ref, count_ref, tiles_ref, *refs):
    *blocks, w_in_ref, w_ref, picked_ref = refs
    place_tiles(picked_ref, *blocks)
    multiply_part(part, list_ref, count_ref, tiles_ref, picked_ref, w_ref)


def last_kernel(list_ref, count_ref, tiles_ref, first_ref, second_ref, w_in_ref, zx_ref, g_ref, w_ref, zw_ref, sums_ref, picked_ref,
                whi_ref):
    place_tiles(picked_ref, first_ref, second_ref)
    multiply_part(4, list_ref, count_ref, tiles_ref, picked_ref, w_ref)
    for t in range(ROWS):
        whi, wlo = split(w_ref[t])
        zw_ref[t * TILE:(t + 1) * TILE, :] = jnp.concatenate([whi, wlo], axis=1)
        whi_ref[:, t * TILE:(t + 1) * TILE] = whi.T
    zw = zw_ref[...]
    m = jnp.dot(zx_ref[...], zw, preferred_element_type=F32)
    s = jnp.dot(whi_ref[...], zw, preferred_element_type=F32)
    cross = s[:, K:]
    sums_ref[0:K, 0:K] = m[:K, :K] + m[:K, K:] + m[K:, :K]
    row = lax.broadcasted_iota(jnp.int32, (K, K), 0)
    col = lax.broadcasted_iota(jnp.int32, (K, K), 1)
    g = g_ref[...]
    sums_ref[0:K, K:] = jnp.where(col >= row, s[:, :K] + cross + cross.T, g)
    sums_ref[K:, 0:K] = jnp.broadcast_to(jnp.sum(jnp.where(col == row, g, 0.0), axis=0, keepdims=True), (8, K))
    sums_ref[K:, K:] = jnp.zeros((8, K), F32)


def eliminate(blocks):
    shape = blocks[0].shape
    count = len(blocks)
    sub = lax.broadcasted_iota(jnp.int32, shape, 0)
    wide = lambda v: jnp.broadcast_to(v, shape)
    done, pivots = [None] * count, []
    for start in range(0, 8 * count, 4):
        b, o = divmod(start, 8)
        head = blocks[b]
        line = [wide(head[o + j:o + j + 1, :]) for j in range(4)]
        column = [[wide(blocks[i][:, start + j:start + j + 1]) for j in range(4)] for i in range(b, count)]
        a = [[wide(column[0][l][o + j:o + j + 1, :]) for l in range(4)] for j in range(4)]
        inverse, m = [None] * 4, {}
        for j in range(4):
            inverse[j] = 1.0 / a[j][j]
            for t in range(j + 1, 4):
                m[t, j] = a[j][t] * inverse[j]
                for l in range(t, 4):
                    a[t][l] = a[t][l] - m[t, j] * a[j][l]
            for t in range(j + 1, 4):
                line[t] = line[t] - m[t, j] * line[j]
        scaled = [line[j] * inverse[j] for j in range(4)]
        for i in range(b, count):
            if i == b and o == 4:
                continue
            c = column[i - b]
            for j in range(4):
                for t in range(j + 1, 4):
                    c[t] = c[t] - m[t, j] * c[j]
            blocks[i] = blocks[i] - ((c[0] * scaled[0] + c[1] * scaled[1]) + (c[2] * scaled[2] + c[3] * scaled[3]))
        rows = blocks[b] if done[b] is None else done[b]
        for j in range(4):
            rows = jnp.where(sub == o + j, line[j] * lax.rsqrt(a[j][j]), rows)
            pivots.append(a[j][j])
        done[b] = rows
    return done, pivots


def factor_kernel(node_total, sums_ref, rayleigh_ref, r_ref, f_ref, flag_ref):
    inv = 1.0 / node_total
    r = sums_ref[0:K, 0:K] * inv
    both = sums_ref[0:K, K:] * inv
    diagonal = sums_ref[K:K + 1, 0:K] * inv
    row = lax.broadcasted_iota(jnp.int32, (K, K), 0)
    col = lax.broadcasted_iota(jnp.int32, (K, K), 1)
    eye = jnp.where(row == col, 1.0, 0.0)
    rt = r.T
    flip = both.T
    s = jnp.where(col >= row, both, flip)
    g = jnp.where(col < row, both, jnp.where(col > row, flip, diagonal))
    gram = s - dot3(rt, dot3(2.0 * eye - g, r))
    work = jnp.concatenate([gram, eye], axis=1)
    done, pivots = eliminate([work[8 * b:8 * b + 8] for b in range(K // 8)])
    work = jnp.concatenate(done, axis=0)
    lower_inv = jnp.where(col <= row, work[:, K:], 0.0)
    rayleigh_ref[...] = r
    r_ref[...] = jnp.where(col >= row, work[:, :K], 0.0)
    f_ref[:, 0:K] = lower_inv
    f_ref[:, K:] = -dot3(lower_inv, rt)
    largest = jnp.max(jnp.where(row == col, s, 0.0))
    smallest = jnp.min(functools.reduce(jnp.minimum, pivots))
    flag_ref[0] = jnp.where(smallest * WORST >= largest, 0, 1).astype(jnp.int32)


def final_kernel(f_ref, zw_ref, zx_ref, r_ref, out_hbm, r_hbm, out_ref, sems):
    copies = [pltpu.make_async_copy(r_ref, r_hbm, sems.at[CHUNKS])]
    copies[0].start()
    f1h, f1l = split(f_ref[:, 0:K])
    f2h, f2l = split(f_ref[:, K:])
    zero = jnp.zeros((K, K), BF16)
    left = [jnp.concatenate([jnp.concatenate([hi, hi], axis=1), jnp.concatenate([lo, zero], axis=1)], axis=0)
            for hi, lo in ((f1h, f1l), (f2h, f2l))]
    wide = NODES_DEV // CHUNKS
    for c in range(CHUNKS):
        lanes = slice(c * wide, (c + 1) * wide)
        y = (lax.dot_general(left[0], zw_ref[lanes, :], NT, preferred_element_type=F32)
             + jnp.dot(left[1], zx_ref[:, lanes], preferred_element_type=F32))
        out_ref[:, lanes] = y[:K] + y[K:]
        copies.append(pltpu.make_async_copy(out_ref.at[:, lanes], out_hbm.at[:, lanes], sems.at[c]))
        copies[-1].start()
    for copy in copies:
        copy.wait()


def exchange(v, axis, to):
    n = lax.axis_size(axis)
    return lax.ppermute(v, axis, [(i, to(i)) for i in range(n)])


def core_swap(v):
    return exchange(v, "row", lambda i: i ^ 1)


def onward(v, way):
    return exchange(v, "row", lambda i: (i + (2 * way if i % 2 == 0 else -2 * way)) % 8)


def total(v):
    v = v + core_swap(v)
    for axis, unit in (("row", 2), ("col", 4), ("col", 1)):
        others = {d: exchange(v, axis, lambda i, d=d * unit: i ^ d) for d in (1, 2, 3)}
        v = (v + others[2]) + (others[3] + others[1])
    return v


def local(tile_blocks, tile_column, row_degree, node_weight, block_now, block_prev, coupling):
    node_total = NODES_DEV * lax.axis_size("row") * lax.axis_size("col")
    after = lax.optimization_barrier
    w_vmem = pltpu.VMEM(NODE_ROWS, F32)
    pair_vmem = pltpu.VMEM((2 * K, NODES_DEV), BF16)
    picked = lambda n: pltpu.VMEM((1 + n * ROWS, K, TILE), BF16)
    square = jax.ShapeDtypeStruct((K, K), F32)

    half, x = call(
        round_kernel, "round_block", (pltpu.VMEM(SLAB, BF16), pltpu.VMEM((K, NODES_DEV), F32)), [hbm()],
        (vmem(), vmem()), 8, 1, [pltpu.SemaphoreType.DMA((4,))])(in_hbm(block_now.T))
    a1 = onward(half, 1)
    a2 = onward(half, -1)
    tiles, w, zx, g, lists, counts = call(
        prepare_kernel, "prepare",
        (pltpu.VMEM((SLOTS, TILE, TILE), BF16), w_vmem, pair_vmem, pltpu.VMEM((K, K), F32),
         pltpu.SMEM((1, TABLE), jnp.int32), pltpu.SMEM((PARTS,), jnp.int32)),
        [hbm()] * 6 + [vmem()] * 2, (vmem(), vmem(), vmem(), vmem(), smem(), smem()), 16, 9,
        [pltpu.VMEM((1, SLOTS), jnp.int32), pltpu.VMEM((1, ROWS), jnp.int32), pltpu.VMEM((K, NODES_DEV), F32),
         pltpu.VMEM((1, NODES_DEV), F32), pltpu.VMEM((K, K), F32), pltpu.VMEM((1, TABLE), jnp.int32),
         picked(1), pltpu.SemaphoreType.DMA((6,)), pltpu.SemaphoreType.DMA((CHUNKS,))])(
            in_hbm(tile_blocks), in_hbm(tile_column.reshape(1, SLOTS)), in_hbm(row_degree.reshape(1, ROWS)),
            in_hbm(block_prev.T), in_hbm(node_weight.reshape(1, NODES_DEV)), in_hbm(coupling), x, half)

    def add_part(part, name, blocks, w, us):
        n = len(blocks)
        slabs = sum(block.shape[0] for block in blocks) // ROWS
        return call(functools.partial(part_kernel, part), name, w_vmem, [smem(), smem()] + [vmem()] * (n + 2),
                    vmem(), 12, us, [picked(slabs)], {3 + n: 0})(
                        lists, counts, tiles, *blocks, w)

    a1, w = after((a1, w))
    h = ROWS // 2
    f1 = onward(a1[:h], 1)
    f2 = onward(a2[h:], -1)
    half, w = after((half, w))
    sib = core_swap(half)
    b1 = core_swap(a1)
    b2 = core_swap(a2)
    w = add_part(1, "near_part", [a1, a2, sib], w, 8)
    w = add_part(2, "near_swapped", [b1, b2], w, 0)
    f1, f2, w = after((f1, f2, w))
    s1 = core_swap(f1)
    s2 = core_swap(f2)
    w = add_part(3, "far_part", [f1, f2], w, 2)
    _, zw, sums = call(
        last_kernel, "last_part", (w_vmem, pltpu.VMEM((NODES_DEV, 2 * K), BF16), jax.ShapeDtypeStruct((K + 8, 2 * K), F32)),
        [smem(), smem()] + [vmem()] * 6, (vmem(), vmem(), vmem()), 16, 4,
        [picked(1), pltpu.VMEM((K, NODES_DEV), BF16)], {5: 0})(lists, counts, tiles, s1, s2, w, zx, g)

    sums = total(sums)
    rayleigh, r_factor, f, flag = call(
        functools.partial(factor_kernel, node_total), "factor",
        (square, square, jax.ShapeDtypeStruct((K, 2 * K), F32), pltpu.SMEM((1,), jnp.int32)),
        [vmem()], (vmem(), vmem(), vmem(), smem()), 8, 5)(sums)

    def plain(zw, zx, f, sums, r_factor):
        return call(
            final_kernel, "scale_block", (pltpu.HBM((K, NODES_DEV), F32), pltpu.HBM((K, K), F32)), [vmem()] * 4,
            (hbm(), hbm()), 12, 2, [pltpu.VMEM((K, NODES_DEV), F32), pltpu.SemaphoreType.DMA((CHUNKS + 1,))])(
                f, zw, zx, r_factor)

    def two_passes(zw, zx, f, sums, r_factor):
        whole = lambda z: z[:K].astype(F32) + z[K:].astype(F32)
        zw = zw.T
        rayleigh_t = sums[:K, :K].T / node_total
        w_next = whole(zw) - jnp.dot(rayleigh_t, whole(zx), precision=HIGHEST)
        gram = total(jnp.dot(w_next, w_next.T, precision=HIGHEST)) / node_total
        lower = jnp.linalg.cholesky(gram)
        return jax.scipy.linalg.solve_triangular(lower, w_next, lower=True), lower.T

    out, r_factor = lax.cond(flag[0] == 0, plain, two_passes, zw, zx, f, sums, r_factor)
    return out.T, rayleigh, r_factor


def solution(mesh):
    in_specs = (
        P(("row", "col"), None, None),
        P(("row", "col")),
        P(("row", "col")),
        P(("row", "col")),
        P(("row", "col"), None),
        P(("row", "col"), None),
        P(),
    )
    out_specs = (P(("row", "col"), None), P(), P())
    return jax.shard_map(local, mesh=mesh, in_specs=in_specs, out_specs=out_specs, check_vma=False)
```

```python
import functools
import jax
import jax.numpy as jnp
from jax import lax
from jax.experimental import pallas as pl
from jax.experimental.pallas import tpu as pltpu
from jax.sharding import PartitionSpec as P

TILE = 128
K = 64
ROWS = 32
SLOTS = 512
NODES_DEV = ROWS * TILE
UNROLL = 16
LIST = 614
PARTS = 5
TABLE = 3072
CHUNKS = 8
WORST = 32.0
F32 = jnp.float32
BF16 = jnp.bfloat16
NT = (((1,), (1,)), ((), ()))
HIGHEST = lax.Precision.HIGHEST
SLAB = (ROWS, K, TILE)
NODE_ROWS = (ROWS, TILE, K)


def vmem():
    return pl.BlockSpec(memory_space=pltpu.VMEM)


def smem():
    return pl.BlockSpec(memory_space=pltpu.SMEM)


def hbm():
    return pl.BlockSpec(memory_space=pltpu.HBM)


def in_hbm(x):
    return pltpu.with_memory_space_constraint(x, pltpu.HBM)


def call(kernel, name, out_shape, in_specs, out_specs, mib, us, scratch=(), aliases=None):
    return pl.pallas_call(
        kernel, out_shape=out_shape, in_specs=in_specs, out_specs=out_specs, scratch_shapes=list(scratch), name=name,
        input_output_aliases=aliases or {},
        compiler_params=pltpu.CompilerParams(vmem_limit_bytes=mib << 20),
        cost_estimate=pl.CostEstimate(flops=int(us * 1e9), bytes_accessed=int(us * 3e6), transcendentals=0))


def split(x):
    hi = x.astype(BF16)
    return hi, (x - hi.astype(F32)).astype(BF16)


def split3(x):
    hi, rest = x.astype(BF16), x - x.astype(BF16).astype(F32)
    mid = rest.astype(BF16)
    return hi, mid, (rest - mid.astype(F32)).astype(BF16)


def dot3(a, b):
    ah, al = split(a)
    bh, bl = split(b)
    return jnp.dot(jnp.concatenate([ah, ah, al], axis=1), jnp.concatenate([bh, bl, bh], axis=0),
                   preferred_element_type=F32)


def round_kernel(x_hbm, half_ref, x_ref, sems):
    wide = NODES_DEV // 4
    copies = [pltpu.make_async_copy(x_hbm.at[:, c * wide:(c + 1) * wide], x_ref.at[:, c * wide:(c + 1) * wide],
                                    sems.at[c]) for c in range(4)]
    for copy in copies:
        copy.start()
    for c, copy in enumerate(copies):
        copy.wait()
        for t in range(c * wide // TILE, (c + 1) * wide // TILE):
            half_ref[t] = x_ref[:, t * TILE:(t + 1) * TILE].astype(BF16)


def build_lists(column, degree, table_ref, count_ref):
    member_row = lax.axis_index("row")
    z = lax.shift_right_logical(member_row, 1)
    core = member_row & 1
    from_z = (z + 3 + 2 * core) & 3
    peer = lax.shift_right_logical(column, 9)
    peer_z = lax.shift_right_logical(peer, 1)
    dz = (peer_z - z) & 3
    dc = (peer & 1) ^ core
    side = jnp.where(peer_z == from_z, 1, 0)
    odd = (dz & 1) == 1
    part = jnp.where(odd, 1 + dc, jnp.where(dz == 0, dc, 3 + dc))
    offset = jnp.where(odd, jnp.where(side == dc, 32, 0), jnp.where(dz == 0, 64 * dc, 0))
    tile = 1 + (column & 31) + offset
    r_i = lax.broadcasted_iota(jnp.int32, (ROWS, ROWS), 0)
    r_j = lax.broadcasted_iota(jnp.int32, (ROWS, ROWS), 1)
    degrees = jnp.broadcast_to(degree, (ROWS, ROWS))
    starts = jnp.sum(jnp.where(r_j < r_i, degrees, 0), axis=1, keepdims=True)
    ends = jnp.sum(jnp.where(r_j <= r_i, degrees, 0), axis=1, keepdims=True)
    s = lax.broadcasted_iota(jnp.int32, (ROWS, SLOTS), 1)
    member = jnp.where((s >= starts) & (s < ends), 1.0, 0.0)
    row = jnp.sum(member * lax.broadcasted_iota(jnp.int32, (ROWS, SLOTS), 0).astype(F32), axis=0, keepdims=True)
    used = jnp.sum(member, axis=0, keepdims=True)
    member = member.astype(BF16)
    line = lax.broadcasted_iota(jnp.int32, (8, SLOTS), 0)
    mine = jnp.where((line == part) & (used > 0.5), 1.0, 0.0)
    mine_half = mine.astype(BF16)
    s_i = lax.broadcasted_iota(jnp.int32, (SLOTS, SLOTS), 0)
    s_j = lax.broadcasted_iota(jnp.int32, (SLOTS, SLOTS), 1)
    before = jnp.where(s_i < s_j, 1.0, 0.0).astype(BF16)
    rank = jnp.dot(mine_half, before, preferred_element_type=F32)
    per_row = lax.dot_general(mine_half, member, NT, preferred_element_type=F32).astype(jnp.int32)
    pad = per_row & 1
    earlier = jnp.where(r_i < r_j, 1.0, 0.0).astype(BF16)
    pads = jnp.dot(pad.astype(F32).astype(BF16), earlier, preferred_element_type=F32)
    shift = jnp.dot(pads.astype(BF16), member, preferred_element_type=F32)
    base = (line * LIST).astype(F32)
    place = (jnp.sum(mine * (rank + shift + base + 1.0), axis=0, keepdims=True) - 1.0).astype(jnp.int32)
    slot = lax.broadcasted_iota(jnp.int32, (1, SLOTS), 1)
    values = jnp.where(line == 0, tile, jnp.where(line == 1, slot & 31, jnp.where(
        line == 2, lax.shift_right_logical(slot, 5), row.astype(jnp.int32))))
    values = values.astype(F32).astype(BF16)
    for c in range(TABLE // 256):
        at = lax.broadcasted_iota(jnp.int32, (256, SLOTS), 0) + c * 256
        hot = jnp.where(at == place, 1.0, 0.0).astype(BF16)
        got = lax.dot_general(values, hot, NT, preferred_element_type=F32).astype(jnp.int32)
        table_ref[0:1, c * 256:(c + 1) * 256] = got[0:1] | (got[1:2] << 10) | (got[2:3] << 15) | (got[3:4] << 20)
    length = jnp.sum(per_row + pad, axis=1, keepdims=True)
    first = lax.broadcasted_iota(jnp.int32, (8, 1), 0)
    for p in range(PARTS):
        n = jnp.sum(jnp.where(first == p, length, 0))
        count_ref[p] = lax.div(n + 2 * UNROLL - 1, 2 * UNROLL)


def multiply_part(part, list_ref, count_ref, tiles_ref, picked_ref, w_ref):
    def group(g, carry):
        base = part * LIST + g * (2 * UNROLL)
        rows, products = [], []
        for u in range(UNROLL):
            first, second = list_ref[0, base + 2 * u], list_ref[0, base + 2 * u + 1]
            x = [picked_ref[e & 255] for e in (first, second)]
            a = [tiles_ref[lax.shift_right_logical(e, 10) & 511] for e in (first, second)]
            rows.append(lax.shift_right_logical(first, 20))
            products.append(lax.dot_general(
                jnp.concatenate(a, axis=1), jnp.concatenate(x, axis=1), NT, preferred_element_type=F32))
        for row, product in zip(rows, products):
            w_ref[row] += product
        return carry

    lax.fori_loop(0, count_ref[part], group, 0)


def place_tiles(picked_ref, *blocks):
    picked_ref[0] = jnp.zeros((K, TILE), BF16)
    at = 1
    for block in blocks:
        picked_ref[at:at + block.shape[0]] = block[...]
        at += block.shape[0]


def tile_copies(tiles_hbm, tiles_ref, sems):
    n = SLOTS // CHUNKS
    spans = [slice(c * n, (c + 1) * n) for c in range(CHUNKS)]
    return [pltpu.make_async_copy(tiles_hbm.at[span], tiles_ref.at[span], sems.at[c]) for c, span in enumerate(spans)]


def prepare_kernel(tiles_hbm, column_hbm, degree_hbm, prev_hbm, weight_hbm, coupling_hbm, x_ref,
                   half_ref, tiles_ref, w_ref, zx_ref, g_ref, list_ref, count_ref,
                   column_ref, degree_ref, prev_ref, weight_ref, coupling_ref, table_ref, picked_ref, sems,
                   tile_sems):
    small = [pltpu.make_async_copy(a, b, sems.at[i]) for i, (a, b) in enumerate((
        (column_hbm, column_ref), (degree_hbm, degree_ref), (coupling_hbm, coupling_ref), (weight_hbm, weight_ref),
        (prev_hbm, prev_ref)))]
    large = tile_copies(tiles_hbm, tiles_ref, tile_sems)
    for copy in small + large:
        copy.start()
    small[0].wait()
    small[1].wait()
    build_lists(column_ref[...], degree_ref[...], table_ref, count_ref)
    table = pltpu.make_async_copy(table_ref, list_ref, sems.at[5])
    table.start()
    for copy in small[2:]:
        copy.wait()
    chi, clo = split(coupling_ref[...])
    left = jnp.concatenate([chi, chi, clo], axis=1)
    wide = 512
    for c in range(NODES_DEV // wide):
        lanes = slice(c * wide, (c + 1) * wide)
        x = x_ref[:, lanes]
        for i, part in enumerate(split3(x)):
            zx_ref[i * K:(i + 1) * K, lanes] = part
        phi, plo = split(prev_ref[:, lanes])
        coupled = jnp.dot(left, jnp.concatenate([phi, plo, phi], axis=0), preferred_element_type=F32)
        w = x * weight_ref[:, lanes] - coupled
        for t in range(wide // TILE):
            w_ref[c * (wide // TILE) + t] = w[:, t * TILE:(t + 1) * TILE].T
    zx = zx_ref[0:2 * K, :]
    gg = lax.dot_general(zx[:K], zx, NT, preferred_element_type=F32)
    cross = gg[:, K:]
    g_ref[...] = gg[:, :K] + cross + cross.T
    place_tiles(picked_ref, half_ref)
    table.wait()
    for copy in large:
        copy.wait()
    multiply_part(0, list_ref, count_ref, tiles_ref, picked_ref, w_ref)


def part_kernel(part, list_ref, count_ref, tiles_ref, *refs):
    *blocks, w_in_ref, w_ref, picked_ref = refs
    place_tiles(picked_ref, *blocks)
    multiply_part(part, list_ref, count_ref, tiles_ref, picked_ref, w_ref)


def last_kernel(list_ref, count_ref, tiles_ref, first_ref, second_ref, w_in_ref, zx_ref, g_ref, w_ref, zw_ref, sums_ref, picked_ref):
    place_tiles(picked_ref, first_ref, second_ref)
    multiply_part(4, list_ref, count_ref, tiles_ref, picked_ref, w_ref)
    for t in range(ROWS):
        for i, part in enumerate(split3(w_ref[t].T)):
            zw_ref[i * K:(i + 1) * K, t * TILE:(t + 1) * TILE] = part
    zw = zw_ref[0:2 * K, :]
    m = lax.dot_general(zx_ref[0:2 * K, :], zw, NT, preferred_element_type=F32)
    s = lax.dot_general(zw[:K], zw, NT, preferred_element_type=F32)
    cross = s[:, K:]
    sums_ref[0:K, 0:K] = m[:K, :K] + m[:K, K:] + m[K:, :K]
    row = lax.broadcasted_iota(jnp.int32, (K, K), 0)
    col = lax.broadcasted_iota(jnp.int32, (K, K), 1)
    g = g_ref[...]
    sums_ref[0:K, K:] = jnp.where(col >= row, s[:, :K] + cross + cross.T, g)
    sums_ref[K:, 0:K] = jnp.broadcast_to(jnp.sum(jnp.where(col == row, g, 0.0), axis=0, keepdims=True), (8, K))
    sums_ref[K:, K:] = jnp.zeros((8, K), F32)


def eliminate(blocks):
    shape = blocks[0].shape
    count = len(blocks)
    sub = lax.broadcasted_iota(jnp.int32, shape, 0)
    wide = lambda v: jnp.broadcast_to(v, shape)
    done, pivots = [None] * count, []
    for start in range(0, 8 * count, 4):
        b, o = divmod(start, 8)
        head = blocks[b]
        line = [wide(head[o + j:o + j + 1, :]) for j in range(4)]
        column = [[wide(blocks[i][:, start + j:start + j + 1]) for j in range(4)] for i in range(b, count)]
        a = [[wide(column[0][l][o + j:o + j + 1, :]) for l in range(4)] for j in range(4)]
        inverse, m = [None] * 4, {}
        for j in range(4):
            inverse[j] = 1.0 / a[j][j]
            for t in range(j + 1, 4):
                m[t, j] = a[j][t] * inverse[j]
                for l in range(t, 4):
                    a[t][l] = a[t][l] - m[t, j] * a[j][l]
            for t in range(j + 1, 4):
                line[t] = line[t] - m[t, j] * line[j]
        scaled = [line[j] * inverse[j] for j in range(4)]
        for i in range(b, count):
            if i == b and o == 4:
                continue
            c = column[i - b]
            for j in range(4):
                for t in range(j + 1, 4):
                    c[t] = c[t] - m[t, j] * c[j]
            blocks[i] = blocks[i] - ((c[0] * scaled[0] + c[1] * scaled[1]) + (c[2] * scaled[2] + c[3] * scaled[3]))
        rows = blocks[b] if done[b] is None else done[b]
        for j in range(4):
            rows = jnp.where(sub == o + j, line[j] * lax.rsqrt(a[j][j]), rows)
            pivots.append(a[j][j])
        done[b] = rows
    return done, pivots


def factor_kernel(node_total, sums_ref, rayleigh_ref, r_ref, f_ref, flag_ref):
    inv = 1.0 / node_total
    r = sums_ref[0:K, 0:K] * inv
    both = sums_ref[0:K, K:] * inv
    diagonal = sums_ref[K:K + 1, 0:K] * inv
    row = lax.broadcasted_iota(jnp.int32, (K, K), 0)
    col = lax.broadcasted_iota(jnp.int32, (K, K), 1)
    eye = jnp.where(row == col, 1.0, 0.0)
    turned = sums_ref[0:K, :].T * inv
    rt, flip = turned[:K], turned[K:]
    s = jnp.where(col >= row, both, flip)
    g = jnp.where(col < row, both, jnp.where(col > row, flip, diagonal))
    gram = s - dot3(rt, dot3(2.0 * eye - g, r))
    work = jnp.concatenate([gram, eye], axis=1)
    done, pivots = eliminate([work[8 * b:8 * b + 8] for b in range(K // 8)])
    work = jnp.concatenate(done, axis=0)
    lower_inv = jnp.where(col <= row, work[:, K:], 0.0)
    rayleigh_ref[...] = r
    r_ref[...] = jnp.where(col >= row, work[:, :K], 0.0)
    f_ref[:, 0:K] = lower_inv
    f_ref[:, K:] = -dot3(lower_inv, rt)
    largest = jnp.max(jnp.where(row == col, s, 0.0))
    smallest = jnp.min(functools.reduce(jnp.minimum, pivots))
    flag_ref[0] = jnp.where(smallest * WORST >= largest, 0, 1).astype(jnp.int32)


def final_kernel(f_ref, zw_ref, zx_ref, r_ref, out_hbm, r_hbm, out_ref, sems):
    copies = [pltpu.make_async_copy(r_ref, r_hbm, sems.at[CHUNKS])]
    copies[0].start()
    f1h, f1l = split(f_ref[:, 0:K])
    f2h, f2l = split(f_ref[:, K:])
    zero = jnp.zeros((K, K), BF16)
    left = jnp.concatenate([jnp.concatenate([f1h, f1h, f2h, f2h], axis=1),
                            jnp.concatenate([f1l, zero, f2l, zero], axis=1)], axis=0)
    wide = NODES_DEV // CHUNKS
    for c in range(CHUNKS):
        lanes = slice(c * wide, (c + 1) * wide)
        z = jnp.concatenate([zw_ref[0:2 * K, lanes], zx_ref[0:2 * K, lanes]], axis=0)
        y = jnp.dot(left, z, preferred_element_type=F32)
        out_ref[:, lanes] = y[:K] + y[K:]
        copies.append(pltpu.make_async_copy(out_ref.at[:, lanes], out_hbm.at[:, lanes], sems.at[c]))
        copies[-1].start()
    for copy in copies:
        copy.wait()


def exchange(v, axis, to):
    n = lax.axis_size(axis)
    return lax.ppermute(v, axis, [(i, to(i)) for i in range(n)])


def core_swap(v):
    return exchange(v, "row", lambda i: i ^ 1)


def onward(v, way):
    return exchange(v, "row", lambda i: (i + (2 * way if i % 2 == 0 else -2 * way)) % 8)


def total(v):
    v = v + core_swap(v)
    for axis, unit in (("row", 2), ("col", 4), ("col", 1)):
        others = {d: exchange(v, axis, lambda i, d=d * unit: i ^ d) for d in (1, 2, 3)}
        v = (v + others[2]) + (others[3] + others[1])
    return v


def local(tile_blocks, tile_column, row_degree, node_weight, block_now, block_prev, coupling):
    node_total = NODES_DEV * lax.axis_size("row") * lax.axis_size("col")
    after = lax.optimization_barrier
    w_vmem = pltpu.VMEM(NODE_ROWS, F32)
    parts_vmem = pltpu.VMEM((3 * K, NODES_DEV), BF16)
    picked = lambda n: pltpu.VMEM((1 + n * ROWS, K, TILE), BF16)
    square = jax.ShapeDtypeStruct((K, K), F32)

    half, x = call(
        round_kernel, "round_block", (pltpu.VMEM(SLAB, BF16), pltpu.VMEM((K, NODES_DEV), F32)), [hbm()],
        (vmem(), vmem()), 8, 1, [pltpu.SemaphoreType.DMA((4,))])(in_hbm(block_now.T))
    a1 = onward(half, 1)
    a2 = onward(half, -1)
    tiles, w, zx, g, lists, counts = call(
        prepare_kernel, "prepare",
        (pltpu.VMEM((SLOTS, TILE, TILE), BF16), w_vmem, parts_vmem, pltpu.VMEM((K, K), F32),
         pltpu.SMEM((1, TABLE), jnp.int32), pltpu.SMEM((PARTS,), jnp.int32)),
        [hbm()] * 6 + [vmem()] * 2, (vmem(), vmem(), vmem(), vmem(), smem(), smem()), 16, 9,
        [pltpu.VMEM((1, SLOTS), jnp.int32), pltpu.VMEM((1, ROWS), jnp.int32), pltpu.VMEM((K, NODES_DEV), F32),
         pltpu.VMEM((1, NODES_DEV), F32), pltpu.VMEM((K, K), F32), pltpu.VMEM((1, TABLE), jnp.int32),
         picked(1), pltpu.SemaphoreType.DMA((6,)), pltpu.SemaphoreType.DMA((CHUNKS,))])(
            in_hbm(tile_blocks), in_hbm(tile_column.reshape(1, SLOTS)), in_hbm(row_degree.reshape(1, ROWS)),
            in_hbm(block_prev.T), in_hbm(node_weight.reshape(1, NODES_DEV)), in_hbm(coupling), x, half)

    def add_part(part, name, blocks, w, us):
        n = len(blocks)
        slabs = sum(block.shape[0] for block in blocks) // ROWS
        return call(functools.partial(part_kernel, part), name, w_vmem, [smem(), smem()] + [vmem()] * (n + 2),
                    vmem(), 12, us, [picked(slabs)], {3 + n: 0})(
                        lists, counts, tiles, *blocks, w)

    a1, w = after((a1, w))
    h = ROWS // 2
    f1 = onward(a1[:h], 1)
    f2 = onward(a2[h:], -1)
    half, w = after((half, w))
    sib = core_swap(half)
    b1 = core_swap(a1)
    b2 = core_swap(a2)
    w = add_part(1, "near_part", [a1, a2, sib], w, 8)
    w = add_part(2, "near_swapped", [b1, b2], w, 0)
    f1, f2, w = after((f1, f2, w))
    s1 = core_swap(f1)
    s2 = core_swap(f2)
    w = add_part(3, "far_part", [f1, f2], w, 2)
    _, zw, sums = call(
        last_kernel, "last_part", (w_vmem, parts_vmem, jax.ShapeDtypeStruct((K + 8, 2 * K), F32)),
        [smem(), smem()] + [vmem()] * 6, (vmem(), vmem(), vmem()), 16, 4,
        [picked(1)], {5: 0})(lists, counts, tiles, s1, s2, w, zx, g)

    sums = total(sums)
    rayleigh, r_factor, f, flag = call(
        functools.partial(factor_kernel, node_total), "factor",
        (square, square, jax.ShapeDtypeStruct((K, 2 * K), F32), pltpu.SMEM((1,), jnp.int32)),
        [vmem()], (vmem(), vmem(), vmem(), smem()), 8, 5)(sums)

    def plain(zw, zx, f, sums, r_factor):
        return call(
            final_kernel, "scale_block", (pltpu.HBM((K, NODES_DEV), F32), pltpu.HBM((K, K), F32)), [vmem()] * 4,
            (hbm(), hbm()), 12, 2, [pltpu.VMEM((K, NODES_DEV), F32), pltpu.SemaphoreType.DMA((CHUNKS + 1,))])(
                f, zw, zx, r_factor)

    def two_passes(zw, zx, f, sums, r_factor):
        rayleigh_t = sums[:K, :K].T / node_total
        whole = lambda z: (z[:K].astype(F32) + z[K:2 * K].astype(F32)) + z[2 * K:].astype(F32)
        w_next = whole(zw) - jnp.dot(rayleigh_t, whole(zx), precision=HIGHEST)
        gram = total(jnp.dot(w_next, w_next.T, precision=HIGHEST)) / node_total
        lower = jnp.linalg.cholesky(gram)
        return jax.scipy.linalg.solve_triangular(lower, w_next, lower=True), lower.T

    out, r_factor = lax.cond(flag[0] == 0, plain, two_passes, zw, zx, f, sums, r_factor)
    return out.T, rayleigh, r_factor


def solution(mesh):
    in_specs = (
        P(("row", "col"), None, None),
        P(("row", "col")),
        P(("row", "col")),
        P(("row", "col")),
        P(("row", "col"), None),
        P(("row", "col"), None),
        P(),
    )
    out_specs = (P(("row", "col"), None), P(), P())
    return jax.shard_map(local, mesh=mesh, in_specs=in_specs, out_specs=out_specs, check_vma=False)
```

```python
import functools
import jax
import jax.numpy as jnp
from jax import lax
from jax.experimental import pallas as pl
from jax.experimental.pallas import tpu as pltpu
from jax.sharding import PartitionSpec as P

TILE = 128
K = 64
ROWS = 32
SLOTS = 512
NODES_DEV = ROWS * TILE
UNROLL = 16
LIST = 614
PARTS = 5
TABLE = 3072
CHUNKS = 8
WORST = 32.0
F32 = jnp.float32
BF16 = jnp.bfloat16
NT = (((1,), (1,)), ((), ()))
HIGHEST = lax.Precision.HIGHEST
SLAB = (ROWS, K, TILE)
NODE_ROWS = (ROWS, TILE, K)


def vmem():
    return pl.BlockSpec(memory_space=pltpu.VMEM)


def smem():
    return pl.BlockSpec(memory_space=pltpu.SMEM)


def hbm():
    return pl.BlockSpec(memory_space=pltpu.HBM)


def in_hbm(x):
    return pltpu.with_memory_space_constraint(x, pltpu.HBM)


def call(kernel, name, out_shape, in_specs, out_specs, mib, us, scratch=(), aliases=None):
    return pl.pallas_call(
        kernel, out_shape=out_shape, in_specs=in_specs, out_specs=out_specs, scratch_shapes=list(scratch), name=name,
        input_output_aliases=aliases or {},
        compiler_params=pltpu.CompilerParams(vmem_limit_bytes=mib << 20),
        cost_estimate=pl.CostEstimate(flops=int(us * 1e9), bytes_accessed=int(us * 3e6), transcendentals=0))


def split(x):
    hi = x.astype(BF16)
    return hi, (x - hi.astype(F32)).astype(BF16)


def split3(x):
    hi, rest = x.astype(BF16), x - x.astype(BF16).astype(F32)
    mid = rest.astype(BF16)
    return hi, mid, (rest - mid.astype(F32)).astype(BF16)


def dot3(a, b):
    ah, al = split(a)
    bh, bl = split(b)
    return jnp.dot(jnp.concatenate([ah, ah, al], axis=1), jnp.concatenate([bh, bl, bh], axis=0),
                   preferred_element_type=F32)


def round_kernel(x_hbm, half_ref, x_ref, sems):
    wide = NODES_DEV // 4
    copies = [pltpu.make_async_copy(x_hbm.at[:, c * wide:(c + 1) * wide], x_ref.at[:, c * wide:(c + 1) * wide],
                                    sems.at[c]) for c in range(4)]
    for copy in copies:
        copy.start()
    for c, copy in enumerate(copies):
        copy.wait()
        for t in range(c * wide // TILE, (c + 1) * wide // TILE):
            half_ref[t] = x_ref[:, t * TILE:(t + 1) * TILE].astype(BF16)


def build_lists(column, degree, table_ref, count_ref):
    member_row = lax.axis_index("row")
    z = lax.shift_right_logical(member_row, 1)
    core = member_row & 1
    from_z = (z + 3 + 2 * core) & 3
    peer = lax.shift_right_logical(column, 9)
    peer_z = lax.shift_right_logical(peer, 1)
    dz = (peer_z - z) & 3
    dc = (peer & 1) ^ core
    side = jnp.where(peer_z == from_z, 1, 0)
    odd = (dz & 1) == 1
    part = jnp.where(odd, 1 + dc, jnp.where(dz == 0, dc, 3 + dc))
    offset = jnp.where(odd, jnp.where(side == dc, 32, 0), jnp.where(dz == 0, 64 * dc, 0))
    tile = 1 + (column & 31) + offset
    r_i = lax.broadcasted_iota(jnp.int32, (ROWS, ROWS), 0)
    r_j = lax.broadcasted_iota(jnp.int32, (ROWS, ROWS), 1)
    degrees = jnp.broadcast_to(degree, (ROWS, ROWS))
    starts = jnp.sum(jnp.where(r_j < r_i, degrees, 0), axis=1, keepdims=True)
    ends = jnp.sum(jnp.where(r_j <= r_i, degrees, 0), axis=1, keepdims=True)
    s = lax.broadcasted_iota(jnp.int32, (ROWS, SLOTS), 1)
    member = jnp.where((s >= starts) & (s < ends), 1.0, 0.0)
    row = jnp.sum(member * lax.broadcasted_iota(jnp.int32, (ROWS, SLOTS), 0).astype(F32), axis=0, keepdims=True)
    used = jnp.sum(member, axis=0, keepdims=True)
    member = member.astype(BF16)
    line = lax.broadcasted_iota(jnp.int32, (8, SLOTS), 0)
    mine = jnp.where((line == part) & (used > 0.5), 1.0, 0.0)
    mine_half = mine.astype(BF16)
    s_i = lax.broadcasted_iota(jnp.int32, (SLOTS, SLOTS), 0)
    s_j = lax.broadcasted_iota(jnp.int32, (SLOTS, SLOTS), 1)
    before = jnp.where(s_i < s_j, 1.0, 0.0).astype(BF16)
    rank = jnp.dot(mine_half, before, preferred_element_type=F32)
    per_row = lax.dot_general(mine_half, member, NT, preferred_element_type=F32).astype(jnp.int32)
    pad = per_row & 1
    earlier = jnp.where(r_i < r_j, 1.0, 0.0).astype(BF16)
    pads = jnp.dot(pad.astype(F32).astype(BF16), earlier, preferred_element_type=F32)
    shift = jnp.dot(pads.astype(BF16), member, preferred_element_type=F32)
    base = (line * LIST).astype(F32)
    place = (jnp.sum(mine * (rank + shift + base + 1.0), axis=0, keepdims=True) - 1.0).astype(jnp.int32)
    slot = lax.broadcasted_iota(jnp.int32, (1, SLOTS), 1)
    values = jnp.where(line == 0, tile, jnp.where(line == 1, slot & 31, jnp.where(
        line == 2, lax.shift_right_logical(slot, 5), row.astype(jnp.int32))))
    values = values.astype(F32).astype(BF16)
    for c in range(TABLE // 256):
        at = lax.broadcasted_iota(jnp.int32, (256, SLOTS), 0) + c * 256
        hot = jnp.where(at == place, 1.0, 0.0).astype(BF16)
        got = lax.dot_general(values, hot, NT, preferred_element_type=F32).astype(jnp.int32)
        table_ref[0:1, c * 256:(c + 1) * 256] = got[0:1] | (got[1:2] << 10) | (got[2:3] << 15) | (got[3:4] << 20)
    length = jnp.sum(per_row + pad, axis=1, keepdims=True)
    first = lax.broadcasted_iota(jnp.int32, (8, 1), 0)
    for p in range(PARTS):
        n = jnp.sum(jnp.where(first == p, length, 0))
        count_ref[p] = lax.div(n + 2 * UNROLL - 1, 2 * UNROLL)


def multiply_part(part, list_ref, count_ref, tiles_ref, picked_ref, w_ref):
    def group(g, carry):
        base = part * LIST + g * (2 * UNROLL)
        rows, products = [], []
        for u in range(UNROLL):
            first, second = list_ref[0, base + 2 * u], list_ref[0, base + 2 * u + 1]
            x = [picked_ref[e & 255] for e in (first, second)]
            a = [tiles_ref[lax.shift_right_logical(e, 10) & 511] for e in (first, second)]
            rows.append(lax.shift_right_logical(first, 20))
            products.append(lax.dot_general(
                jnp.concatenate(a, axis=1), jnp.concatenate(x, axis=1), NT, preferred_element_type=F32))
        for row, product in zip(rows, products):
            w_ref[row] += product
        return carry

    lax.fori_loop(0, count_ref[part], group, 0)


def place_tiles(picked_ref, *blocks):
    picked_ref[0] = jnp.zeros((K, TILE), BF16)
    at = 1
    for block in blocks:
        picked_ref[at:at + block.shape[0]] = block[...]
        at += block.shape[0]


def tile_copies(tiles_hbm, tiles_ref, sems):
    n = SLOTS // CHUNKS
    spans = [slice(c * n, (c + 1) * n) for c in range(CHUNKS)]
    return [pltpu.make_async_copy(tiles_hbm.at[span], tiles_ref.at[span], sems.at[c]) for c, span in enumerate(spans)]


def prepare_kernel(tiles_hbm, column_hbm, degree_hbm, prev_hbm, weight_hbm, coupling_hbm, x_ref,
                   half_ref, tiles_ref, w_ref, zx_ref, g_ref, list_ref, count_ref,
                   column_ref, degree_ref, prev_ref, weight_ref, coupling_ref, table_ref, picked_ref, sems,
                   tile_sems):
    small = [pltpu.make_async_copy(a, b, sems.at[i]) for i, (a, b) in enumerate((
        (column_hbm, column_ref), (degree_hbm, degree_ref), (coupling_hbm, coupling_ref), (weight_hbm, weight_ref),
        (prev_hbm, prev_ref)))]
    large = tile_copies(tiles_hbm, tiles_ref, tile_sems)
    for copy in small + large:
        copy.start()
    small[0].wait()
    small[1].wait()
    build_lists(column_ref[...], degree_ref[...], table_ref, count_ref)
    table = pltpu.make_async_copy(table_ref, list_ref, sems.at[5])
    table.start()
    for copy in small[2:]:
        copy.wait()
    chi, clo = split(coupling_ref[...])
    left = jnp.concatenate([chi, chi, clo], axis=1)
    wide = 512
    for c in range(NODES_DEV // wide):
        lanes = slice(c * wide, (c + 1) * wide)
        x = x_ref[:, lanes]
        for i, part in enumerate(split3(x)):
            zx_ref[i * K:(i + 1) * K, lanes] = part
        phi, plo = split(prev_ref[:, lanes])
        coupled = jnp.dot(left, jnp.concatenate([phi, plo, phi], axis=0), preferred_element_type=F32)
        w = x * weight_ref[:, lanes] - coupled
        for t in range(wide // TILE):
            w_ref[c * (wide // TILE) + t] = w[:, t * TILE:(t + 1) * TILE].T
    zx = zx_ref[0:2 * K, :]
    gg = lax.dot_general(zx[:K], zx, NT, preferred_element_type=F32)
    cross = gg[:, K:]
    g_ref[...] = gg[:, :K] + cross + cross.T
    place_tiles(picked_ref, half_ref)
    table.wait()
    for copy in large:
        copy.wait()
    multiply_part(0, list_ref, count_ref, tiles_ref, picked_ref, w_ref)


def part_kernel(part, list_ref, count_ref, tiles_ref, *refs):
    *blocks, w_in_ref, w_ref, picked_ref = refs
    place_tiles(picked_ref, *blocks)
    multiply_part(part, list_ref, count_ref, tiles_ref, picked_ref, w_ref)


def last_kernel(list_ref, count_ref, tiles_ref, first_ref, second_ref, w_in_ref, zx_ref, g_ref, w_ref, zw_ref, sums_ref, picked_ref):
    place_tiles(picked_ref, first_ref, second_ref)
    multiply_part(4, list_ref, count_ref, tiles_ref, picked_ref, w_ref)
    for t in range(ROWS):
        for i, part in enumerate(split3(w_ref[t].T)):
            zw_ref[i * K:(i + 1) * K, t * TILE:(t + 1) * TILE] = part
    zw = zw_ref[0:2 * K, :]
    m = lax.dot_general(zx_ref[0:2 * K, :], zw, NT, preferred_element_type=F32)
    s = lax.dot_general(zw[:K], zw, NT, preferred_element_type=F32)
    cross = s[:, K:]
    sums_ref[0:K, 0:K] = m[:K, :K] + m[:K, K:] + m[K:, :K]
    row = lax.broadcasted_iota(jnp.int32, (K, K), 0)
    col = lax.broadcasted_iota(jnp.int32, (K, K), 1)
    g = g_ref[...]
    sums_ref[0:K, K:] = jnp.where(col >= row, s[:, :K] + cross + cross.T, g)
    sums_ref[K:, 0:K] = jnp.broadcast_to(jnp.sum(jnp.where(col == row, g, 0.0), axis=0, keepdims=True), (8, K))
    sums_ref[K:, K:] = jnp.zeros((8, K), F32)


def eliminate(blocks):
    shape = blocks[0].shape
    count = len(blocks)
    sub = lax.broadcasted_iota(jnp.int32, shape, 0)
    wide = lambda v: jnp.broadcast_to(v, shape)
    done, pivots = [None] * count, []
    for start in range(0, 8 * count, 4):
        b, o = divmod(start, 8)
        head = blocks[b]
        line = [wide(head[o + j:o + j + 1, :]) for j in range(4)]
        column = [[wide(blocks[i][:, start + j:start + j + 1]) for j in range(4)] for i in range(b, count)]
        a = [[wide(column[0][l][o + j:o + j + 1, :]) for l in range(4)] for j in range(4)]
        inverse, m = [None] * 4, {}
        for j in range(4):
            inverse[j] = 1.0 / a[j][j]
            for t in range(j + 1, 4):
                m[t, j] = a[j][t] * inverse[j]
                for l in range(t, 4):
                    a[t][l] = a[t][l] - m[t, j] * a[j][l]
            for t in range(j + 1, 4):
                line[t] = line[t] - m[t, j] * line[j]
        scaled = [line[j] * inverse[j] for j in range(4)]
        for i in range(b, count):
            if i == b and o == 4:
                continue
            c = column[i - b]
            for j in range(4):
                for t in range(j + 1, 4):
                    c[t] = c[t] - m[t, j] * c[j]
            blocks[i] = blocks[i] - ((c[0] * scaled[0] + c[1] * scaled[1]) + (c[2] * scaled[2] + c[3] * scaled[3]))
        rows = blocks[b] if done[b] is None else done[b]
        for j in range(4):
            rows = jnp.where(sub == o + j, line[j] * lax.rsqrt(a[j][j]), rows)
            pivots.append(a[j][j])
        done[b] = rows
    return done, pivots


def factor_kernel(node_total, sums_ref, rayleigh_ref, r_ref, f_ref, flag_ref):
    inv = 1.0 / node_total
    r = sums_ref[0:K, 0:K] * inv
    both = sums_ref[0:K, K:] * inv
    diagonal = sums_ref[K:K + 1, 0:K] * inv
    row = lax.broadcasted_iota(jnp.int32, (K, K), 0)
    col = lax.broadcasted_iota(jnp.int32, (K, K), 1)
    eye = jnp.where(row == col, 1.0, 0.0)
    turned = sums_ref[0:K, :].T * inv
    rt, flip = turned[:K], turned[K:]
    s = jnp.where(col >= row, both, flip)
    g = jnp.where(col < row, both, jnp.where(col > row, flip, diagonal))
    gram = s - dot3(rt, dot3(2.0 * eye - g, r))
    work = jnp.concatenate([gram, eye], axis=1)
    done, pivots = eliminate([work[8 * b:8 * b + 8] for b in range(K // 8)])
    work = jnp.concatenate(done, axis=0)
    lower_inv = jnp.where(col <= row, work[:, K:], 0.0)
    rayleigh_ref[...] = r
    r_ref[...] = jnp.where(col >= row, work[:, :K], 0.0)
    f_ref[:, 0:K] = lower_inv
    f_ref[:, K:] = -dot3(lower_inv, rt)
    largest = jnp.max(jnp.where(row == col, s, 0.0))
    smallest = jnp.min(functools.reduce(jnp.minimum, pivots))
    flag_ref[0] = jnp.where(smallest * WORST >= largest, 0, 1).astype(jnp.int32)


def final_kernel(f_ref, zw_ref, zx_ref, r_ref, out_hbm, r_hbm, out_ref, sems):
    copies = [pltpu.make_async_copy(r_ref, r_hbm, sems.at[CHUNKS])]
    copies[0].start()
    f1h, f1l = split(f_ref[:, 0:K])
    f2h, f2l = split(f_ref[:, K:])
    zero = jnp.zeros((K, K), BF16)
    left = jnp.concatenate([jnp.concatenate([f1h, f1h, f2h, f2h], axis=1),
                            jnp.concatenate([f1l, zero, f2l, zero], axis=1)], axis=0)
    wide = NODES_DEV // CHUNKS
    for c in range(CHUNKS):
        lanes = slice(c * wide, (c + 1) * wide)
        z = jnp.concatenate([zw_ref[0:2 * K, lanes], zx_ref[0:2 * K, lanes]], axis=0)
        y = jnp.dot(left, z, preferred_element_type=F32)
        out_ref[:, lanes] = y[:K] + y[K:]
        copies.append(pltpu.make_async_copy(out_ref.at[:, lanes], out_hbm.at[:, lanes], sems.at[c]))
        copies[-1].start()
    for copy in copies:
        copy.wait()


def exchange(v, axis, to):
    n = lax.axis_size(axis)
    return lax.ppermute(v, axis, [(i, to(i)) for i in range(n)])


def core_swap(v):
    return exchange(v, "row", lambda i: i ^ 1)


def onward(v, way):
    return exchange(v, "row", lambda i: (i + (2 * way if i % 2 == 0 else -2 * way)) % 8)


def total(v):
    v = v + core_swap(v)
    for axis, unit in (("row", 2), ("col", 4), ("col", 1)):
        others = {d: exchange(v, axis, lambda i, d=d * unit: i ^ d) for d in (1, 2, 3)}
        if axis == "row":
            v = (v + others[2]) + (others[1] + others[3])
        else:
            v = (v + others[2]) + (others[3] + others[1])
    return v


def local(tile_blocks, tile_column, row_degree, node_weight, block_now, block_prev, coupling):
    node_total = NODES_DEV * lax.axis_size("row") * lax.axis_size("col")
    after = lax.optimization_barrier
    w_vmem = pltpu.VMEM(NODE_ROWS, F32)
    parts_vmem = pltpu.VMEM((3 * K, NODES_DEV), BF16)
    picked = lambda n: pltpu.VMEM((1 + n * ROWS, K, TILE), BF16)
    square = jax.ShapeDtypeStruct((K, K), F32)

    half, x = call(
        round_kernel, "round_block", (pltpu.VMEM(SLAB, BF16), pltpu.VMEM((K, NODES_DEV), F32)), [hbm()],
        (vmem(), vmem()), 8, 1, [pltpu.SemaphoreType.DMA((4,))])(in_hbm(block_now.T))
    a1 = onward(half, 1)
    a2 = onward(half, -1)
    tiles, w, zx, g, lists, counts = call(
        prepare_kernel, "prepare",
        (pltpu.VMEM((SLOTS, TILE, TILE), BF16), w_vmem, parts_vmem, pltpu.VMEM((K, K), F32),
         pltpu.SMEM((1, TABLE), jnp.int32), pltpu.SMEM((PARTS,), jnp.int32)),
        [hbm()] * 6 + [vmem()] * 2, (vmem(), vmem(), vmem(), vmem(), smem(), smem()), 16, 9,
        [pltpu.VMEM((1, SLOTS), jnp.int32), pltpu.VMEM((1, ROWS), jnp.int32), pltpu.VMEM((K, NODES_DEV), F32),
         pltpu.VMEM((1, NODES_DEV), F32), pltpu.VMEM((K, K), F32), pltpu.VMEM((1, TABLE), jnp.int32),
         picked(1), pltpu.SemaphoreType.DMA((6,)), pltpu.SemaphoreType.DMA((CHUNKS,))])(
            in_hbm(tile_blocks), in_hbm(tile_column.reshape(1, SLOTS)), in_hbm(row_degree.reshape(1, ROWS)),
            in_hbm(block_prev.T), in_hbm(node_weight.reshape(1, NODES_DEV)), in_hbm(coupling), x, half)

    def add_part(part, name, blocks, w, us):
        n = len(blocks)
        slabs = sum(block.shape[0] for block in blocks) // ROWS
        return call(functools.partial(part_kernel, part), name, w_vmem, [smem(), smem()] + [vmem()] * (n + 2),
                    vmem(), 12, us, [picked(slabs)], {3 + n: 0})(
                        lists, counts, tiles, *blocks, w)

    a1, w = after((a1, w))
    h = ROWS // 2
    f1 = onward(a1[:h], 1)
    f2 = onward(a2[h:], -1)
    half, w = after((half, w))
    sib = core_swap(half)
    b1 = core_swap(a1)
    b2 = core_swap(a2)
    w = add_part(1, "near_part", [a1, a2, sib], w, 8)
    w = add_part(2, "near_swapped", [b1, b2], w, 0)
    f1, f2, w = after((f1, f2, w))
    s1 = core_swap(f1)
    s2 = core_swap(f2)
    w = add_part(3, "far_part", [f1, f2], w, 2)
    _, zw, sums = call(
        last_kernel, "last_part", (w_vmem, parts_vmem, jax.ShapeDtypeStruct((K + 8, 2 * K), F32)),
        [smem(), smem()] + [vmem()] * 6, (vmem(), vmem(), vmem()), 16, 4,
        [picked(1)], {5: 0})(lists, counts, tiles, s1, s2, w, zx, g)

    sums = total(sums)
    rayleigh, r_factor, f, flag = call(
        functools.partial(factor_kernel, node_total), "factor",
        (square, square, jax.ShapeDtypeStruct((K, 2 * K), F32), pltpu.SMEM((1,), jnp.int32)),
        [vmem()], (vmem(), vmem(), vmem(), smem()), 8, 5)(sums)

    def plain(zw, zx, f, sums, r_factor):
        return call(
            final_kernel, "scale_block", (pltpu.HBM((K, NODES_DEV), F32), pltpu.HBM((K, K), F32)), [vmem()] * 4,
            (hbm(), hbm()), 12, 2, [pltpu.VMEM((K, NODES_DEV), F32), pltpu.SemaphoreType.DMA((CHUNKS + 1,))])(
                f, zw, zx, r_factor)

    def two_passes(zw, zx, f, sums, r_factor):
        rayleigh_t = sums[:K, :K].T / node_total
        whole = lambda z: (z[:K].astype(F32) + z[K:2 * K].astype(F32)) + z[2 * K:].astype(F32)
        w_next = whole(zw) - jnp.dot(rayleigh_t, whole(zx), precision=HIGHEST)
        gram = total(jnp.dot(w_next, w_next.T, precision=HIGHEST)) / node_total
        lower = jnp.linalg.cholesky(gram)
        return jax.scipy.linalg.solve_triangular(lower, w_next, lower=True), lower.T

    out, r_factor = lax.cond(flag[0] == 0, plain, two_passes, zw, zx, f, sums, r_factor)
    return out.T, rayleigh, r_factor


def solution(mesh):
    in_specs = (
        P(("row", "col"), None, None),
        P(("row", "col")),
        P(("row", "col")),
        P(("row", "col")),
        P(("row", "col"), None),
        P(("row", "col"), None),
        P(),
    )
    out_specs = (P(("row", "col"), None), P(), P())
    return jax.shard_map(local, mesh=mesh, in_specs=in_specs, out_specs=out_specs, check_vma=False)
```
